256 devices in a mesh: lon: 32 (over x_hi, z, core), lat: 8 (over x_lo, y).
Axes of the slice: x: 4 (x_hi: 2, x_lo: 2; x = x_hi * 2 + x_lo), y: 4, z: 8, core: 2. Of those that a mesh axis runs over, the one named last changes fastest.
Arguments:
- tokens: bfloat16 [384, 96, 4, 512], P('lon', 'lat'), may hold values from -6 to 6
- grad_out: bfloat16 [384, 96, 4, 512], P('lon', 'lat'), may hold values from -6 to 6
- norm1_gain: bfloat16 [512], replicated, may hold values from 0.099609375 to 1.8984375
- qkv_weight: bfloat16 [512, 1536], replicated
- proj_weight: bfloat16 [512, 512], replicated, may hold values from -0.25 to 0.25
- norm2_gain: bfloat16 [512], replicated, may hold values from 0.099609375 to 1.8984375
- up_weight: bfloat16 [512, 2048], replicated, may hold values from -0.25 to 0.25
- down_weight: bfloat16 [2048, 512], replicated, may hold values from -0.125 to 0.125
Outputs:
- output: bfloat16 [384, 96, 4, 512], P('lon', 'lat')
- token_grad: bfloat16 [384, 96, 4, 512], P('lon', 'lat')
The draws below stay inside these ranges and needn't reach their ends.
All inputs are finite; a program needn't handle non-finite values.
Results may differ from the reference program's by a relative error of at most 0.013.
Values may be sent and summed in bfloat16 or wider, within the bound.
A program may use at most 128 MiB of HBM per device.

```python
import math
import jax
import jax.numpy as jnp
from jax import lax

D = 512
HEADS = 8
FF = 2048
LEVELS = 4
WLON = 12
WLAT = 6
WLEV = 2
NLON = 384
NLAT = 96


def draw_qkv_weight(key, part):
    key = jax.random.fold_in(key, 7)
    base_draw = jax.random.normal(key, (D, 3 * D), jnp.float32) * D ** (-0.5)
    return base_draw.astype(jnp.bfloat16)


def levels(key, shape, cuts, low, largest):
    loudness = 1.0
    for position, blocks in cuts:
        steps = jax.random.uniform(jax.random.fold_in(jax.random.fold_in(key, 6), position), (blocks,), jnp.float32, low / len(cuts), largest / len(cuts))
        loudness = loudness * jnp.repeat(jnp.exp(steps), shape[position] // blocks).reshape((-1,) + (1,) * (len(shape) - 1 - position))
    return loudness


def scatter_about(own_key, dims, scale, most, cuts=(), dtype=jnp.bfloat16):
    loudness = levels(own_key, dims, cuts, -0.22, 0.18) if cuts else 1.0
    entries = jax.random.normal(own_key, dims, jnp.float32) * scale * loudness
    return jnp.minimum(jnp.maximum(entries, -most), most).astype(dtype)


def setup_inputs(seed: int = 0) -> dict:
    key_of = jax.random.split(jax.random.key(seed), 9)
    tokens = scatter_about(key_of[0], (NLON, NLAT, LEVELS, D), 1.0, 6.0, ((0, 32), (1, 8)))
    grad_out = scatter_about(key_of[1], (NLON, NLAT, LEVELS, D), 1.0, 6.0, ((0, 32), (1, 8)))
    norm1_gain = jnp.clip(1.0 + 0.18 * jax.random.normal(key_of[2], (D,), jnp.float32), 0.099609375, 1.8984375).astype(jnp.bfloat16)
    qkv_weight = draw_qkv_weight(jax.random.fold_in(key_of[8], 71), 0)
    proj_weight = scatter_about(key_of[4], (D, D), D ** -0.5, 0.25)
    norm2_gain = jnp.clip(1.0 + 0.18 * jax.random.normal(key_of[5], (D,), jnp.float32), 0.099609375, 1.8984375).astype(jnp.bfloat16)
    up_weight = scatter_about(key_of[6], (D, FF), D ** -0.5, 0.25)
    down_weight = scatter_about(key_of[7], (FF, D), FF ** -0.5, 0.125)
    return {"tokens": tokens, "grad_out": grad_out, "norm1_gain": norm1_gain, "qkv_weight": qkv_weight, "proj_weight": proj_weight, "norm2_gain": norm2_gain, "up_weight": up_weight, "down_weight": down_weight}


EPS = 1e-05

def layer_norm(values, gain_vec):
    as_float = values.astype(jnp.float32)
    centre = as_float - lax.optimization_barrier(jnp.mean(as_float, -1, keepdims=True))
    inv_std = lax.rsqrt(lax.optimization_barrier(jnp.mean(centre * centre, -1, keepdims=True)) + EPS)
    unit = centre * inv_std
    return (unit * gain_vec.astype(jnp.float32), unit, inv_std)

def norm_grad(upstream, unit, inv_std, gain_vec):
    scaled = upstream * gain_vec.astype(jnp.float32)
    return inv_std * (scaled - lax.optimization_barrier(jnp.mean(scaled, -1, keepdims=True)) - unit * lax.optimization_barrier(jnp.mean(scaled * unit, -1, keepdims=True)))

def gelu_tanh(values):
    return jax.nn.gelu(values, approximate=True)

def matmul(left, right):
    flat = left.reshape(-1, left.shape[-1])
    return jnp.dot(flat, right, preferred_element_type=jnp.float32).reshape(left.shape[:-1] + (right.shape[-1],))

def to_windows(grid):
    span_a, span_b, span_c, chans = grid.shape
    split = grid.reshape(span_a // WLON, WLON, span_b // WLAT, WLAT, span_c // WLEV, WLEV, chans)
    return split.transpose(0, 2, 4, 1, 3, 5, 6).reshape(-1, WLON * WLAT * WLEV, chans)

def from_windows(blocks, span_a, span_b, span_c):
    chans = blocks.shape[-1]
    split = blocks.reshape(span_a // WLON, span_b // WLAT, span_c // WLEV, WLON, WLAT, WLEV, chans)
    return split.transpose(0, 3, 1, 4, 2, 5, 6).reshape(span_a, span_b, span_c, chans)

def window_mask(lat_rows, lat_total, span_a, span_c):
    lat_part = (lat_rows >= lat_total - WLAT // 2).astype(jnp.int32)
    lev_part = (jnp.arange(span_c) >= span_c - WLEV // 2).astype(jnp.int32)
    label = lat_part[:, None] * 2 + lev_part[None, :]
    label = jnp.broadcast_to(label[None, :, :, None], (span_a, lat_rows.shape[0], span_c, 1))
    flat = to_windows(label)[:, :, 0]
    return flat[:, :, None] == flat[:, None, :]

def split_heads(qkv_blocks, heads):
    count, wsize, triple = qkv_blocks.shape
    head_dim = triple // 3 // heads
    split = qkv_blocks.astype(jnp.float32).reshape(count, wsize, 3, heads, head_dim)
    return (split[:, :, 0], split[:, :, 1], split[:, :, 2], head_dim)

def attend(qkv_blocks, allowed, heads):
    count, wsize, triple = qkv_blocks.shape
    queries, key_rows, value_rows, head_dim = split_heads(qkv_blocks, heads)
    scores = jnp.einsum('nqhe,nkhe->nhqk', queries, key_rows) / math.sqrt(head_dim)
    scores = jnp.where(allowed[:, None], scores, -1e+30)
    expo = jnp.exp(scores - lax.optimization_barrier(jnp.max(scores, -1, keepdims=True)))
    probs = expo / lax.optimization_barrier(jnp.sum(expo, -1, keepdims=True))
    rounded = lax.optimization_barrier(probs.astype(jnp.bfloat16)).astype(jnp.float32)
    mixed = jnp.einsum('nhqk,nkhe->nqhe', rounded, value_rows)
    return (mixed.reshape(count, wsize, triple // 3).astype(jnp.bfloat16), probs)

def attend_grad(qkv_blocks, probs, grad_blocks, heads):
    count, wsize, triple = qkv_blocks.shape
    queries, key_rows, value_rows, head_dim = split_heads(qkv_blocks, heads)
    upstream = grad_blocks.astype(jnp.float32).reshape(count, wsize, heads, head_dim)
    rounded = lax.optimization_barrier(probs.astype(jnp.bfloat16)).astype(jnp.float32)
    grad_prob = jnp.einsum('nqhe,nkhe->nhqk', upstream, value_rows)
    grad_value = jnp.einsum('nhqk,nqhe->nkhe', rounded, upstream)
    grad_score = probs * (grad_prob - lax.optimization_barrier(jnp.sum(grad_prob * probs, -1, keepdims=True)))
    grad_score = lax.optimization_barrier(grad_score.astype(jnp.bfloat16)).astype(jnp.float32)
    grad_query = jnp.einsum('nhqk,nkhe->nqhe', grad_score, key_rows) / math.sqrt(head_dim)
    grad_key = jnp.einsum('nhqk,nqhe->nkhe', grad_score, queries) / math.sqrt(head_dim)
    stacked = jnp.stack([grad_query, grad_key, grad_value], 2)
    return stacked.reshape(count, wsize, triple).astype(jnp.bfloat16)

def reference(tokens, grad_out, norm1_gain, qkv_weight, proj_weight, norm2_gain, up_weight, down_weight):
    span_a, span_b, span_c, width = tokens.shape
    forward_roll = (-(WLON // 2), -(WLAT // 2), -(WLEV // 2))
    back_roll = (WLON // 2, WLAT // 2, WLEV // 2)
    allowed = window_mask(jnp.arange(span_b).astype(jnp.int32), span_b, span_a, span_c)
    normed, unit_one, inv_one = layer_norm(tokens, norm1_gain)
    qkv_all = matmul(normed.astype(jnp.bfloat16), qkv_weight).astype(jnp.bfloat16)
    qkv_blocks = to_windows(jnp.roll(qkv_all, forward_roll, (0, 1, 2)))
    attended, probs = attend(qkv_blocks, allowed, HEADS)
    attended = jnp.roll(from_windows(attended, span_a, span_b, span_c), back_roll, (0, 1, 2))
    mid = (tokens.astype(jnp.float32) + matmul(attended, proj_weight)).astype(jnp.bfloat16)
    normed_two, unit_two, inv_two = layer_norm(mid, norm2_gain)
    hidden_pre = matmul(normed_two.astype(jnp.bfloat16), up_weight)
    activated = gelu_tanh(hidden_pre).astype(jnp.bfloat16)
    output = (mid.astype(jnp.float32) + matmul(activated, down_weight)).astype(jnp.bfloat16)
    grad_hidden = matmul(grad_out, down_weight.T)
    grad_pre = jax.vjp(gelu_tanh, hidden_pre)[1](grad_hidden)[0].astype(jnp.bfloat16)
    grad_norm_two = matmul(grad_pre, up_weight.T)
    grad_mid = (grad_out.astype(jnp.float32) + norm_grad(grad_norm_two, unit_two, inv_two, norm2_gain)).astype(jnp.bfloat16)
    grad_att = matmul(grad_mid, proj_weight.T).astype(jnp.bfloat16)
    grad_blocks = to_windows(jnp.roll(grad_att, forward_roll, (0, 1, 2)))
    grad_qkv = attend_grad(qkv_blocks, probs, grad_blocks, HEADS)
    grad_qkv = jnp.roll(from_windows(grad_qkv, span_a, span_b, span_c), back_roll, (0, 1, 2))
    grad_normed = matmul(grad_qkv, qkv_weight.T).astype(jnp.bfloat16)
    token_grad = (grad_mid.astype(jnp.float32) + norm_grad(grad_normed.astype(jnp.float32), unit_one, inv_one, norm1_gain)).astype(jnp.bfloat16)
    return (output, token_grad)
```

```python
import functools
import math

import jax
import jax.numpy as jnp
from jax import lax
from jax.experimental import pallas as pl
from jax.experimental.pallas import tpu as pltpu
from jax.sharding import PartitionSpec as P

MESH = pl.DeviceIdType.MESH
F32 = jnp.float32
BF16 = jnp.bfloat16
EPS = 1e-05
LON, LAT, LEV, D = 12, 6, 4, 512
POS = LON * LAT
ROWS = POS * LEV
WIN = ROWS // 2
FF = 2048
PAIR = 128
HALF = 64


def dot(a, b):
    return jnp.dot(a, b, preferred_element_type=F32)


def dot_nt(a, b):
    return lax.dot_general(a, b, (((1,), (1,)), ((), ())), preferred_element_type=F32)


def dot_tn(a, b):
    return lax.dot_general(a, b, (((0,), (0,)), ((), ())), preferred_element_type=F32)


def norm_unit(x):
    centre = x - jnp.mean(x, -1, keepdims=True)
    inv_std = lax.rsqrt(jnp.mean(centre * centre, -1, keepdims=True) + EPS)
    return centre * inv_std, inv_std


def norm_grad(upstream, unit, inv_std, gain):
    scaled = upstream * gain
    return inv_std * (
        scaled
        - jnp.mean(scaled, -1, keepdims=True)
        - unit * jnp.mean(scaled * unit, -1, keepdims=True)
    )


def flat(ref):
    return ref[...].reshape(ROWS, D)


def natural_index(r):
    in_second = (r >= WIN).astype(jnp.int32)
    s = r - in_second * WIN
    odd = lax.rem(s, 2)
    level = jnp.where(in_second == 1, 3 - 3 * odd, 1 + odd)
    return (s // 2) * LEV + level


def kernel(
    nlon,
    nlat,
    tokens,
    grad_out,
    gain1_ref,
    wqkv_h,
    wproj_h,
    gain2_ref,
    wup_h,
    wdown_h,
    out_h,
    tgrad_h,
    wqkv,
    wproj,
    wup,
    wdown,
    perm,
    perm_back,
    bias,
    tok_b,
    gout_b,
    win_tok,
    att_res,
    att_b,
    ga_b,
    win_ga,
    gn_res,
    gn_b,
    stage,
    qkv,
    probs,
    gqkv,
    att,
    gh,
    act,
    gpre,
    gmid,
    wsem,
    lsem,
    osem,
    ssem,
    rsem,
):
    lon = lax.axis_index("lon")
    lat = lax.axis_index("lat")
    east, west = lax.rem(lon + 1, nlon), lax.rem(lon + nlon - 1, nlon)
    north, south = lax.rem(lat + 1, nlat), lax.rem(lat + nlat - 1, nlat)
    to_e, to_n, to_ne = (east, lat), (lon, north), (east, north)
    to_w, to_s, to_sw = (west, lat), (lon, south), (west, south)

    loads = []

    def load(src, dst, sem):
        copy = pltpu.make_async_copy(src, dst, sem)
        copy.start()
        return copy

    go_copies = [
        load(grad_out.at[:, 0:3], gout_b.at[0, :, 0:3], lsem.at[0]),
        load(grad_out.at[:, 9:12], gout_b.at[0, :, 3:6], lsem.at[1]),
        load(grad_out.at[:, 3:9], gout_b.at[1], lsem.at[2]),
    ]
    down_copy = load(wdown_h, wdown, wsem.at[0])
    own_copies = [
        load(tokens.at[6:12, 9:12], win_tok.at[0, 0:6, 0:3], lsem.at[3]),
        load(tokens.at[6:12, 3:9], win_tok.at[1, 0:6], lsem.at[4]),
    ]
    qkv_copy = load(wqkv_h, wqkv, wsem.at[1])
    tok_copies = [
        load(tokens.at[:, 0:3], tok_b.at[0, :, 0:3], lsem.at[5]),
        load(tokens.at[:, 9:12], tok_b.at[0, :, 3:6], lsem.at[6]),
        load(tokens.at[:, 3:9], tok_b.at[1], lsem.at[7]),
    ]
    proj_copy = load(wproj_h, wproj, wsem.at[2])
    up_copy = load(wup_h, wup, wsem.at[3])

    barrier = pltpu.get_barrier_semaphore()
    for device in (to_e, to_n, to_ne, to_w, to_s, to_sw):
        pl.semaphore_signal(barrier, inc=1, device_id=device, device_id_type=MESH)
    pl.semaphore_wait(barrier, 6)

    def send(phase, slot, src, dst, device):
        copy = pltpu.make_async_remote_copy(
            src_ref=src,
            dst_ref=dst,
            send_sem=ssem.at[phase, slot],
            recv_sem=rsem.at[phase, slot],
            device_id=device,
            device_id_type=MESH,
        )
        copy.start()
        return copy

    tok_sends_c = [
        send(0, 0, tokens.at[0:6, 0:3], win_tok.at[0, 6:12, 3:6], to_sw),
        send(0, 1, tokens.at[6:12, 0:3], win_tok.at[0, 0:6, 3:6], to_s),
        send(0, 2, tokens.at[0:6, 9:12], win_tok.at[0, 6:12, 0:3], to_w),
    ]
    tok_sends_l = [send(0, 3, tokens.at[0:6, 3:9], win_tok.at[1, 6:12], to_w)]

    def inward(phase, block, src):
        if block == 0:
            return [
                send(phase, 0, src.at[0, 0:6, 0:3], win_ga.at[0, 6:12, 3:6], to_sw),
                send(phase, 1, src.at[0, 6:12, 0:3], win_ga.at[0, 0:6, 3:6], to_s),
                send(phase, 2, src.at[0, 0:6, 3:6], win_ga.at[0, 6:12, 0:3], to_w),
            ]
        return [send(phase, 3, src.at[1, 0:6], win_ga.at[1, 6:12], to_w)]

    def outward(phase, group, src, dst):
        if group == 0:
            return [
                send(phase, 0, src.at[0, 6:12, 3:6], dst.at[0, 0:6, 0:3], to_ne),
                send(phase, 1, src.at[0, 0:6, 3:6], dst.at[0, 6:12, 0:3], to_n),
                send(phase, 2, src.at[0, 6:12, 0:3], dst.at[0, 0:6, 3:6], to_e),
            ]
        return [send(phase, 3, src.at[1, 6:12], dst.at[1, 0:6], to_e)]

    def keep_outward(group, value, dst):
        if group == 0:
            dst[0, 6:12, 3:6] = value[0:6, 0:3]
        else:
            dst[1, 6:12] = value[0:6]

    rows = lax.broadcasted_iota(jnp.int32, (ROWS, ROWS), 0)
    cols = lax.broadcasted_iota(jnp.int32, (ROWS, ROWS), 1)
    perm[...] = (natural_index(rows) == cols).astype(F32).astype(BF16)
    perm_back[...] = (natural_index(cols) == rows).astype(F32).astype(BF16)
    edge = (lat == nlat - 1).astype(jnp.int32)
    row = lax.broadcasted_iota(jnp.int32, (WIN, WIN), 0)
    col = lax.broadcasted_iota(jnp.int32, (WIN, WIN), 1)
    parity = (lax.rem(row, 2) != lax.rem(col, 2)).astype(jnp.int32)
    half_r = (lax.rem(row // 2, LAT) >= LAT // 2).astype(jnp.int32)
    half_c = (lax.rem(col // 2, LAT) >= LAT // 2).astype(jnp.int32)
    across = (half_r != half_c).astype(jnp.int32) * edge
    blocked = ((across, parity + across), (jnp.zeros_like(parity), parity))
    for group in range(2):
        for window in range(2):
            bias[group, window] = jnp.where(blocked[group][window] > 0, -1e30, 0.0)

    low = lax.broadcasted_iota(jnp.int32, (WIN, PAIR), 1) < HALF
    gain1 = gain1_ref[...].astype(F32)
    gain2 = gain2_ref[...].astype(F32)

    def both(pair):
        zero = jnp.zeros_like(pair)
        return jnp.where(low, pair, zero), jnp.where(low, zero, pair)

    for copy in go_copies:
        copy.wait()
    down_copy.wait()
    for block in range(2):
        rows_out = gout_b[block].reshape(ROWS, D)
        for part in range(4):
            span = slice(part * 512, part * 512 + 512)
            gh[block, :, span] = dot_nt(rows_out, wdown[span, :])
    for copy in own_copies:
        copy.wait()
    qkv_copy.wait()

    def forward(group, arrivals):
        for copy in arrivals:
            copy.wait_recv()
        unit, _ = norm_unit(win_tok[group].reshape(ROWS, D).astype(F32))
        normed = (unit * gain1).astype(BF16)
        normed = dot(perm[...], normed).astype(BF16)
        q = dot(normed, wqkv[:, 0:D]).astype(BF16)
        qkv[group, :, 0:D] = q * jnp.asarray(0.125, BF16)
        qkv[group, :, D : 2 * D] = dot(normed, wqkv[:, D : 2 * D]).astype(BF16)
        qkv[group, :, 2 * D : 3 * D] = dot(normed, wqkv[:, 2 * D : 3 * D]).astype(BF16)

        def window_body(window, carry):
            span = pl.ds(pl.multiple_of(window * WIN, 16), WIN)
            allowed = bias[group, window]
            for pair in range(4):
                lanes = pl.ds(pair * PAIR, PAIR)
                k = qkv[group, span, pl.ds(D + pair * PAIR, PAIR)]
                qs = both(qkv[group, span, lanes])
                vs = both(qkv[group, span, pl.ds(2 * D + pair * PAIR, PAIR)])
                mixed = jnp.zeros((WIN, PAIR), F32)
                for head in range(2):
                    scores = dot_nt(qs[head], k) + allowed
                    expo = jnp.exp(scores - jnp.max(scores, -1, keepdims=True))
                    prob = (expo * (1.0 / jnp.sum(expo, -1, keepdims=True))).astype(BF16)
                    probs[group, window, 2 * pair + head] = prob
                    mixed = mixed + dot(prob, vs[head])
                att[span, lanes] = mixed.astype(BF16)
            return carry

        lax.fori_loop(0, 2, window_body, 0)
        result = dot(perm_back[...], att[...]).astype(BF16).reshape(LON, LAT, LEV, D)
        att_res[group] = result
        keep_outward(group, result, att_b)
        return outward(1, group, att_res, att_b)

    def tail(block, arrivals, out_copies):
        for copy in arrivals:
            copy.wait_recv()
        mixed = dot(att_b[block].reshape(ROWS, D), wproj[...])
        mid = (tok_b[block].reshape(ROWS, D).astype(F32) + mixed).astype(BF16)
        unit, inv_std = norm_unit(mid.astype(F32))
        normed = (unit * gain2).astype(BF16)
        for part in range(4):
            span = slice(part * 512, part * 512 + 512)
            x = dot(normed, wup[:, span])
            c = math.sqrt(2.0 / math.pi)
            square = x * x
            t = jnp.tanh(x * (c + (c * 0.044715) * square))
            cdf = 0.5 + 0.5 * t
            act[:, span] = (x * cdf).astype(BF16)
            slope = cdf + (0.5 * x) * (1.0 - t * t) * (c + (3.0 * c * 0.044715) * square)
            gpre[:, span] = (slope * gh[block, :, span]).astype(BF16)
        grad_normed = dot_nt(gpre[...], wup[...])
        grad_rows = gout_b[block].reshape(ROWS, D).astype(F32)
        grad_mid = (grad_rows + norm_grad(grad_normed, unit, inv_std, gain2)).astype(BF16)
        gmid[block] = grad_mid
        grad_att = dot_nt(grad_mid, wproj[...]).astype(BF16).reshape(LON, LAT, LEV, D)
        ga_b[block] = grad_att
        sends = inward(2, block, ga_b)
        if block == 0:
            win_ga[0, 0:6, 0:3] = grad_att[6:12, 3:6]
        else:
            win_ga[1, 0:6] = grad_att[6:12]
        output = (mid.astype(F32) + dot(act[...], wdown[...])).astype(BF16)
        stage[0, block] = output.reshape(LON, LAT, LEV, D)
        out_copies += store(block, 0, out_h)
        return sends

    def store(block, which, dst):
        if block == 0:
            return [
                load(stage.at[which, 0, :, 0:3], dst.at[:, 0:3], osem.at[which, 0]),
                load(stage.at[which, 0, :, 3:6], dst.at[:, 9:12], osem.at[which, 1]),
            ]
        return [load(stage.at[which, 1], dst.at[:, 3:9], osem.at[which, 2])]

    def backward(group, arrivals):
        for copy in arrivals:
            copy.wait_recv()
        att[...] = dot(perm[...], win_ga[group].reshape(ROWS, D)).astype(BF16)

        def window_body(window, carry):
            span = pl.ds(pl.multiple_of(window * WIN, 16), WIN)
            for pair in range(4):
                lanes = pl.ds(pair * PAIR, PAIR)
                k_lanes = pl.ds(D + pair * PAIR, PAIR)
                v_lanes = pl.ds(2 * D + pair * PAIR, PAIR)
                v = qkv[group, span, v_lanes]
                qs = both(qkv[group, span, lanes])
                ks = both(qkv[group, span, k_lanes])
                gs = both(att[span, lanes])
                grad_q = jnp.zeros((WIN, PAIR), F32)
                grad_k = jnp.zeros((WIN, PAIR), F32)
                grad_v = jnp.zeros((WIN, PAIR), F32)
                for head in range(2):
                    prob = probs[group, window, 2 * pair + head]
                    grad_prob = dot_nt(gs[head], v)
                    wide = prob.astype(F32)
                    total = jnp.sum(grad_prob * wide, -1, keepdims=True)
                    grad_score = (wide * (grad_prob - total)).astype(BF16)
                    grad_v = grad_v + dot_tn(prob, gs[head])
                    grad_q = grad_q + dot(grad_score, ks[head])
                    grad_k = grad_k + dot_tn(grad_score, qs[head])
                gqkv[span, lanes] = (grad_q * 0.125).astype(BF16)
                gqkv[span, k_lanes] = grad_k.astype(BF16)
                gqkv[span, v_lanes] = grad_v.astype(BF16)
            return carry

        lax.fori_loop(0, 2, window_body, 0)
        grad_normed = dot_nt(gqkv[...], wqkv[...]).astype(BF16)
        result = dot(perm_back[...], grad_normed).astype(BF16).reshape(LON, LAT, LEV, D)
        gn_res[group] = result
        keep_outward(group, result, gn_b)
        return outward(3, group, gn_res, gn_b)

    def finish(block, arrivals, out_copies):
        for copy in arrivals:
            copy.wait_recv()
        unit, inv_std = norm_unit(tok_b[block].reshape(ROWS, D).astype(F32))
        upstream = gn_b[block].reshape(ROWS, D).astype(F32)
        total = gmid[block].astype(F32) + norm_grad(upstream, unit, inv_std, gain1)
        stage[1, block] = total.astype(BF16).reshape(LON, LAT, LEV, D)
        out_copies += store(block, 1, tgrad_h)

    out_copies = []
    att_sends_c = forward(0, tok_sends_c)
    att_sends_l = forward(1, tok_sends_l)
    proj_copy.wait()
    up_copy.wait()
    for copy in tok_copies:
        copy.wait()
    ga_sends_c = tail(0, att_sends_c, out_copies)
    ga_sends_l = tail(1, att_sends_l, out_copies)
    gn_sends_c = backward(0, ga_sends_c)
    gn_sends_l = backward(1, ga_sends_l)
    finish(0, gn_sends_c, out_copies)
    finish(1, gn_sends_l, out_copies)
    for copy in tok_sends_c + tok_sends_l + att_sends_c + att_sends_l:
        copy.wait_send()
    for copy in ga_sends_c + ga_sends_l + gn_sends_c + gn_sends_l:
        copy.wait_send()
    for copy in out_copies:
        copy.wait()


def on_device(
    nlon,
    nlat,
    tokens,
    grad_out,
    norm1_gain,
    qkv_weight,
    proj_weight,
    norm2_gain,
    up_weight,
    down_weight,
):
    any_spec = pl.BlockSpec(memory_space=pl.ANY)
    vmem_spec = pl.BlockSpec(memory_space=pltpu.VMEM)
    shape = jax.ShapeDtypeStruct(tokens.shape, BF16)
    block = (2, LON, LAT, LEV, D)
    return pl.pallas_call(
        functools.partial(kernel, nlon, nlat),
        out_shape=(shape, shape),
        in_specs=[any_spec, any_spec, vmem_spec, any_spec, any_spec, vmem_spec, any_spec, any_spec],
        out_specs=(any_spec, any_spec),
        scratch_shapes=[
            pltpu.VMEM((D, 3 * D), BF16),
            pltpu.VMEM((D, D), BF16),
            pltpu.VMEM((D, FF), BF16),
            pltpu.VMEM((FF, D), BF16),
            pltpu.VMEM((ROWS, ROWS), BF16),
            pltpu.VMEM((ROWS, ROWS), BF16),
            pltpu.VMEM((2, 2, WIN, WIN), F32),
            pltpu.VMEM(block, BF16),
            pltpu.VMEM(block, BF16),
            pltpu.VMEM(block, BF16),
            pltpu.VMEM(block, BF16),
            pltpu.VMEM(block, BF16),
            pltpu.VMEM(block, BF16),
            pltpu.VMEM(block, BF16),
            pltpu.VMEM(block, BF16),
            pltpu.VMEM(block, BF16),
            pltpu.VMEM((2,) + block, BF16),
            pltpu.VMEM((2, ROWS, 3 * D), BF16),
            pltpu.VMEM((2, 2, 8, WIN, WIN), BF16),
            pltpu.VMEM((ROWS, 3 * D), BF16),
            pltpu.VMEM((ROWS, D), BF16),
            pltpu.VMEM((2, ROWS, FF), F32),
            pltpu.VMEM((ROWS, FF), BF16),
            pltpu.VMEM((ROWS, FF), BF16),
            pltpu.VMEM((2, ROWS, D), BF16),
            pltpu.SemaphoreType.DMA((4,)),
            pltpu.SemaphoreType.DMA((8,)),
            pltpu.SemaphoreType.DMA((2, 3)),
            pltpu.SemaphoreType.DMA((4, 4)),
            pltpu.SemaphoreType.DMA((4, 4)),
        ],
        compiler_params=pltpu.CompilerParams(
            collective_id=0, has_side_effects=True, vmem_limit_bytes=56 * 1024 * 1024
        ),
        cost_estimate=pl.CostEstimate(
            flops=8_000_000_000, bytes_accessed=9_000_000, transcendentals=2_000_000
        ),
    )(
        tokens,
        grad_out,
        norm1_gain.reshape(1, D),
        qkv_weight,
        proj_weight,
        norm2_gain.reshape(1, D),
        up_weight,
        down_weight,
    )


def solution(mesh):
    grid = P("lon", "lat", None, None)
    return jax.shard_map(
        functools.partial(on_device, mesh.shape["lon"], mesh.shape["lat"]),
        mesh=mesh,
        in_specs=(grid, grid) + (P(),) * 6,
        out_specs=(grid, grid),
        check_vma=False,
    )
```

```python
import functools
import math

import jax
import jax.numpy as jnp
from jax import lax
from jax.experimental import pallas as pl
from jax.experimental.pallas import tpu as pltpu
from jax.sharding import PartitionSpec as P

MESH = pl.DeviceIdType.MESH
F32 = jnp.float32
BF16 = jnp.bfloat16
EPS = 1e-05
LON, LAT, LEV, D = 12, 6, 4, 512
POS = LON * LAT
ROWS = POS * LEV
WIN = ROWS // 2
FF = 2048
PAIR = 128
HALF = 64


def dot(a, b):
    return jnp.dot(a, b, preferred_element_type=F32)


def dot_nt(a, b):
    return lax.dot_general(a, b, (((1,), (1,)), ((), ())), preferred_element_type=F32)


def dot_tn(a, b):
    return lax.dot_general(a, b, (((0,), (0,)), ((), ())), preferred_element_type=F32)


def norm_unit(x):
    centre = x - jnp.mean(x, -1, keepdims=True)
    inv_std = lax.rsqrt(jnp.mean(centre * centre, -1, keepdims=True) + EPS)
    return centre * inv_std, inv_std


def norm_grad(upstream, unit, inv_std, gain):
    scaled = upstream * gain
    return inv_std * (
        scaled
        - jnp.mean(scaled, -1, keepdims=True)
        - unit * jnp.mean(scaled * unit, -1, keepdims=True)
    )


def flat(ref):
    return ref[...].reshape(ROWS, D)


def natural_index(r):
    in_second = (r >= WIN).astype(jnp.int32)
    s = r - in_second * WIN
    odd = lax.rem(s, 2)
    level = jnp.where(in_second == 1, 3 - 3 * odd, 1 + odd)
    return (s // 2) * LEV + level


def kernel(
    nlon,
    nlat,
    tokens,
    grad_out,
    gain1_ref,
    wqkv_h,
    wproj_h,
    gain2_ref,
    wup_h,
    wdown_h,
    out_ref,
    tgrad_ref,
    wqkv,
    wproj,
    wup,
    wdown,
    perm,
    perm_back,
    bias,
    tok_b,
    gout_b,
    win_tok,
    att_res,
    att_b,
    ga_b,
    win_ga,
    gn_res,
    gn_b,
    qkv,
    probs,
    gqkv,
    att,
    gh,
    act,
    gpre,
    gmid,
    wsem,
    lsem,
    ssem,
    rsem,
):
    lon = lax.axis_index("lon")
    lat = lax.axis_index("lat")
    east, west = lax.rem(lon + 1, nlon), lax.rem(lon + nlon - 1, nlon)
    north, south = lax.rem(lat + 1, nlat), lax.rem(lat + nlat - 1, nlat)

    def column(index):
        odd = lax.rem(index, 2)
        near, far = 3 * odd, 3 - 3 * odd
        return near, far, odd * south + (1 - odd) * north

    near, far, far_to = column(lon)
    near_e, far_e, far_to_e = column(east)
    far_from = north + south - far_to
    to_e, to_w = (east, lat), (west, lat)
    to_far, to_from = (lon, far_to), (lon, far_from)
    to_e_far, to_w_from = (east, far_to_e), (west, far_from)

    loads = []

    def load(src, dst, sem):
        copy = pltpu.make_async_copy(src, dst, sem)
        copy.start()
        return copy

    go_copies = [
        load(grad_out.at[:, 0:3], gout_b.at[0, :, 0:3], lsem.at[0]),
        load(grad_out.at[:, 9:12], gout_b.at[0, :, 3:6], lsem.at[1]),
        load(grad_out.at[:, 3:9], gout_b.at[1], lsem.at[2]),
    ]
    down_copy = load(wdown_h, wdown, wsem.at[0])
    own_copies = [
        load(tokens.at[0:6, pl.ds(3 * near, 3)], win_tok.at[0, 6:12, pl.ds(3 - near, 3)], lsem.at[3]),
        load(tokens.at[6:12, 3:9], win_tok.at[1, 0:6], lsem.at[4]),
    ]
    qkv_copy = load(wqkv_h, wqkv, wsem.at[1])
    tok_copies = [
        load(tokens.at[:, 0:3], tok_b.at[0, :, 0:3], lsem.at[5]),
        load(tokens.at[:, 9:12], tok_b.at[0, :, 3:6], lsem.at[6]),
        load(tokens.at[:, 3:9], tok_b.at[1], lsem.at[7]),
    ]
    proj_copy = load(wproj_h, wproj, wsem.at[2])
    up_copy = load(wup_h, wup, wsem.at[3])

    barrier = pltpu.get_barrier_semaphore()
    for device in (to_e, to_w, to_far, to_from, to_e_far, to_w_from):
        pl.semaphore_signal(barrier, inc=1, device_id=device, device_id_type=MESH)
    pl.semaphore_wait(barrier, 6)

    def send(phase, slot, src, dst, device):
        copy = pltpu.make_async_remote_copy(
            src_ref=src,
            dst_ref=dst,
            send_sem=ssem.at[phase, slot],
            recv_sem=rsem.at[phase, slot],
            device_id=device,
            device_id_type=MESH,
        )
        copy.start()
        return copy

    tok_sends_c = [
        send(0, 0, tokens.at[6:12, pl.ds(3 * far_e, 3)], win_tok.at[0, 0:6, pl.ds(3 - far_e, 3)], to_e_far),
        send(0, 1, tokens.at[0:6, pl.ds(3 * far, 3)], win_tok.at[0, 6:12, pl.ds(3 - far, 3)], to_far),
        send(0, 2, tokens.at[6:12, pl.ds(3 * near_e, 3)], win_tok.at[0, 0:6, pl.ds(3 - near_e, 3)], to_e),
    ]
    tok_sends_l = [send(0, 3, tokens.at[0:6, 3:9], win_tok.at[1, 6:12], to_w)]

    def inward(phase, block, src):
        if block == 0:
            return [
                send(phase, 0, src.at[0, 6:12, pl.ds(far_e, 3)], win_ga.at[0, 0:6, pl.ds(3 - far_e, 3)], to_e_far),
                send(phase, 1, src.at[0, 0:6, pl.ds(far, 3)], win_ga.at[0, 6:12, pl.ds(3 - far, 3)], to_far),
                send(phase, 2, src.at[0, 6:12, pl.ds(near_e, 3)], win_ga.at[0, 0:6, pl.ds(3 - near_e, 3)], to_e),
            ]
        return [send(phase, 3, src.at[1, 0:6], win_ga.at[1, 6:12], to_w)]

    def outward(phase, group, src, dst):
        if group == 0:
            return [
                send(phase, 0, src.at[0, 0:6, pl.ds(3 - far, 3)], dst.at[0, 6:12, pl.ds(far, 3)], to_w_from),
                send(phase, 1, src.at[0, 6:12, pl.ds(3 - far, 3)], dst.at[0, 0:6, pl.ds(far, 3)], to_from),
                send(phase, 2, src.at[0, 0:6, pl.ds(3 - near, 3)], dst.at[0, 6:12, pl.ds(near, 3)], to_w),
            ]
        return [send(phase, 3, src.at[1, 6:12], dst.at[1, 0:6], to_e)]

    def keep_outward(group, value, res, dst):
        if group == 0:
            dst[0, 0:6, pl.ds(near, 3)] = res[0, 6:12, pl.ds(3 - near, 3)]
        else:
            dst[1, 6:12] = value[0:6]

    rows = lax.broadcasted_iota(jnp.int32, (ROWS, ROWS), 0)
    cols = lax.broadcasted_iota(jnp.int32, (ROWS, ROWS), 1)
    perm[...] = (natural_index(rows) == cols).astype(F32).astype(BF16)
    perm_back[...] = (natural_index(cols) == rows).astype(F32).astype(BF16)
    odd = lax.rem(lon, 2)
    edge = (lat == odd * (nlat - 1)).astype(jnp.int32)
    row = lax.broadcasted_iota(jnp.int32, (WIN, WIN), 0)
    col = lax.broadcasted_iota(jnp.int32, (WIN, WIN), 1)
    parity = (lax.rem(row, 2) != lax.rem(col, 2)).astype(jnp.int32)
    half_r = (lax.rem(row // 2, LAT) >= LAT // 2).astype(jnp.int32)
    half_c = (lax.rem(col // 2, LAT) >= LAT // 2).astype(jnp.int32)
    across = (half_r != half_c).astype(jnp.int32) * edge
    blocked = ((across, parity + across), (jnp.zeros_like(parity), parity))
    for group in range(2):
        for window in range(2):
            bias[group, window] = jnp.where(blocked[group][window] > 0, -1e30, 0.0)

    low = lax.broadcasted_iota(jnp.int32, (WIN, PAIR), 1) < HALF
    gain1 = gain1_ref[...].astype(F32).reshape(1, D)
    gain2 = gain2_ref[...].astype(F32).reshape(1, D)

    def both(pair):
        zero = jnp.zeros_like(pair)
        return jnp.where(low, pair, zero), jnp.where(low, zero, pair)

    for copy in go_copies:
        copy.wait()
    down_copy.wait()
    for block in range(2):
        rows_out = gout_b[block].reshape(ROWS, D)
        for part in range(4):
            span = slice(part * 512, part * 512 + 512)
            gh[block, :, span] = dot_nt(rows_out, wdown[span, :])
    for copy in own_copies:
        copy.wait()
    qkv_copy.wait()

    def forward(group, arrivals):
        for copy in arrivals:
            copy.wait_recv()
        unit, _ = norm_unit(win_tok[group].reshape(ROWS, D).astype(F32))
        normed = (unit * gain1).astype(BF16)
        normed = dot(perm[...], normed).astype(BF16)
        q = dot(normed, wqkv[:, 0:D]).astype(BF16)
        qkv[group, :, 0:D] = q * jnp.asarray(0.125, BF16)
        qkv[group, :, D : 2 * D] = dot(normed, wqkv[:, D : 2 * D]).astype(BF16)
        qkv[group, :, 2 * D : 3 * D] = dot(normed, wqkv[:, 2 * D : 3 * D]).astype(BF16)

        def window_body(window, carry):
            span = pl.ds(pl.multiple_of(window * WIN, 16), WIN)
            allowed = bias[group, window]
            for pair in range(4):
                lanes = pl.ds(pair * PAIR, PAIR)
                k = qkv[group, span, pl.ds(D + pair * PAIR, PAIR)]
                qs = both(qkv[group, span, lanes])
                vs = both(qkv[group, span, pl.ds(2 * D + pair * PAIR, PAIR)])
                mixed = jnp.zeros((WIN, PAIR), F32)
                for head in range(2):
                    scores = dot_nt(qs[head], k) + allowed
                    expo = jnp.exp(scores - jnp.max(scores, -1, keepdims=True))
                    prob = (expo * (1.0 / jnp.sum(expo, -1, keepdims=True))).astype(BF16)
                    probs[group, window, 2 * pair + head] = prob
                    mixed = mixed + dot(prob, vs[head])
                att[span, lanes] = mixed.astype(BF16)
            return carry

        lax.fori_loop(0, 2, window_body, 0)
        result = dot(perm_back[...], att[...]).astype(BF16).reshape(LON, LAT, LEV, D)
        att_res[group] = result
        keep_outward(group, result, att_res, att_b)
        return outward(1, group, att_res, att_b)

    def tail(block, arrivals):
        for copy in arrivals:
            copy.wait_recv()
        mixed = dot(att_b[block].reshape(ROWS, D), wproj[...])
        mid = (tok_b[block].reshape(ROWS, D).astype(F32) + mixed).astype(BF16)
        unit, inv_std = norm_unit(mid.astype(F32))
        normed = (unit * gain2).astype(BF16)
        for part in range(4):
            span = slice(part * 512, part * 512 + 512)
            x = dot(normed, wup[:, span])
            c = math.sqrt(2.0 / math.pi)
            square = x * x
            t = jnp.tanh(x * (c + (c * 0.044715) * square))
            cdf = 0.5 + 0.5 * t
            act[:, span] = (x * cdf).astype(BF16)
            slope = cdf + (0.5 * x) * (1.0 - t * t) * (c + (3.0 * c * 0.044715) * square)
            gpre[:, span] = (slope * gh[block, :, span]).astype(BF16)
        grad_normed = dot_nt(gpre[...], wup[...])
        grad_rows = gout_b[block].reshape(ROWS, D).astype(F32)
        grad_mid = (grad_rows + norm_grad(grad_normed, unit, inv_std, gain2)).astype(BF16)
        gmid[block] = grad_mid
        grad_att = dot_nt(grad_mid, wproj[...]).astype(BF16).reshape(LON, LAT, LEV, D)
        ga_b[block] = grad_att
        sends = inward(2, block, ga_b)
        if block == 0:
            win_ga[0, 6:12, pl.ds(3 - near, 3)] = ga_b[0, 0:6, pl.ds(near, 3)]
        else:
            win_ga[1, 0:6] = grad_att[6:12]
        output = (mid.astype(F32) + dot(act[...], wdown[...])).astype(BF16)
        store(block, output.reshape(LON, LAT, LEV, D), out_ref)
        return sends

    def store(block, value, dst):
        if block == 0:
            dst[:, 0:3] = value[:, 0:3]
            dst[:, 9:12] = value[:, 3:6]
        else:
            dst[:, 3:9] = value

    def backward(group, arrivals):
        for copy in arrivals:
            copy.wait_recv()
        att[...] = dot(perm[...], win_ga[group].reshape(ROWS, D)).astype(BF16)

        def window_body(window, carry):
            span = pl.ds(pl.multiple_of(window * WIN, 16), WIN)
            for pair in range(4):
                lanes = pl.ds(pair * PAIR, PAIR)
                k_lanes = pl.ds(D + pair * PAIR, PAIR)
                v_lanes = pl.ds(2 * D + pair * PAIR, PAIR)
                v = qkv[group, span, v_lanes]
                qs = both(qkv[group, span, lanes])
                ks = both(qkv[group, span, k_lanes])
                gs = both(att[span, lanes])
                grad_q = jnp.zeros((WIN, PAIR), F32)
                grad_k = jnp.zeros((WIN, PAIR), F32)
                grad_v = jnp.zeros((WIN, PAIR), F32)
                for head in range(2):
                    prob = probs[group, window, 2 * pair + head]
                    grad_prob = dot_nt(gs[head], v)
                    wide = prob.astype(F32)
                    total = jnp.sum(grad_prob * wide, -1, keepdims=True)
                    grad_score = (wide * (grad_prob - total)).astype(BF16)
                    grad_v = grad_v + dot_tn(prob, gs[head])
                    grad_q = grad_q + dot(grad_score, ks[head])
                    grad_k = grad_k + dot_tn(grad_score, qs[head])
                gqkv[span, lanes] = (grad_q * 0.125).astype(BF16)
                gqkv[span, k_lanes] = grad_k.astype(BF16)
                gqkv[span, v_lanes] = grad_v.astype(BF16)
            return carry

        lax.fori_loop(0, 2, window_body, 0)
        grad_normed = dot_nt(gqkv[...], wqkv[...]).astype(BF16)
        result = dot(perm_back[...], grad_normed).astype(BF16).reshape(LON, LAT, LEV, D)
        gn_res[group] = result
        keep_outward(group, result, gn_res, gn_b)
        return outward(3, group, gn_res, gn_b)

    def finish(block, arrivals):
        for copy in arrivals:
            copy.wait_recv()
        unit, inv_std = norm_unit(tok_b[block].reshape(ROWS, D).astype(F32))
        upstream = gn_b[block].reshape(ROWS, D).astype(F32)
        total = gmid[block].astype(F32) + norm_grad(upstream, unit, inv_std, gain1)
        store(block, total.astype(BF16).reshape(LON, LAT, LEV, D), tgrad_ref)

    att_sends_c = forward(0, tok_sends_c)
    att_sends_l = forward(1, tok_sends_l)
    proj_copy.wait()
    up_copy.wait()
    for copy in tok_copies:
        copy.wait()
    ga_sends_c = tail(0, att_sends_c)
    ga_sends_l = tail(1, att_sends_l)
    gn_sends_c = backward(0, ga_sends_c)
    gn_sends_l = backward(1, ga_sends_l)
    finish(0, gn_sends_c)
    finish(1, gn_sends_l)
    for copy in tok_sends_c + tok_sends_l + att_sends_c + att_sends_l:
        copy.wait_send()
    for copy in ga_sends_c + ga_sends_l + gn_sends_c + gn_sends_l:
        copy.wait_send()


def write_out(out_ref, tgrad_ref, out_h, tgrad_h, sem):
    copies = []
    for which, (src, dst) in enumerate(((out_ref, out_h), (tgrad_ref, tgrad_h))):
        for part in range(3):
            span = slice(4 * part, 4 * part + 4)
            copies.append(pltpu.make_async_copy(src.at[span], dst.at[span], sem.at[which, part]))
    for copy in copies:
        copy.start()
    for copy in copies:
        copy.wait()


def on_device(
    nlon,
    nlat,
    tokens,
    grad_out,
    norm1_gain,
    qkv_weight,
    proj_weight,
    norm2_gain,
    up_weight,
    down_weight,
):
    any_spec = pl.BlockSpec(memory_space=pl.ANY)
    vmem_spec = pl.BlockSpec(memory_space=pltpu.VMEM)
    shape = jax.ShapeDtypeStruct(tokens.shape, BF16)
    block = (2, LON, LAT, LEV, D)
    in_vmem = pltpu.VMEM(tokens.shape, BF16)
    results = pl.pallas_call(
        functools.partial(kernel, nlon, nlat),
        out_shape=(in_vmem, in_vmem),
        in_specs=[any_spec, any_spec, vmem_spec, any_spec, any_spec, vmem_spec, any_spec, any_spec],
        out_specs=(vmem_spec, vmem_spec),
        scratch_shapes=[
            pltpu.VMEM((D, 3 * D), BF16),
            pltpu.VMEM((D, D), BF16),
            pltpu.VMEM((D, FF), BF16),
            pltpu.VMEM((FF, D), BF16),
            pltpu.VMEM((ROWS, ROWS), BF16),
            pltpu.VMEM((ROWS, ROWS), BF16),
            pltpu.VMEM((2, 2, WIN, WIN), F32),
            pltpu.VMEM(block, BF16),
            pltpu.VMEM(block, BF16),
            pltpu.VMEM(block, BF16),
            pltpu.VMEM(block, BF16),
            pltpu.VMEM(block, BF16),
            pltpu.VMEM(block, BF16),
            pltpu.VMEM(block, BF16),
            pltpu.VMEM(block, BF16),
            pltpu.VMEM(block, BF16),
            pltpu.VMEM((2, ROWS, 3 * D), BF16),
            pltpu.VMEM((2, 2, 8, WIN, WIN), BF16),
            pltpu.VMEM((ROWS, 3 * D), BF16),
            pltpu.VMEM((ROWS, D), BF16),
            pltpu.VMEM((2, ROWS, FF), F32),
            pltpu.VMEM((ROWS, FF), BF16),
            pltpu.VMEM((ROWS, FF), BF16),
            pltpu.VMEM((2, ROWS, D), BF16),
            pltpu.SemaphoreType.DMA((4,)),
            pltpu.SemaphoreType.DMA((8,)),
            pltpu.SemaphoreType.DMA((4, 4)),
            pltpu.SemaphoreType.DMA((4, 4)),
        ],
        compiler_params=pltpu.CompilerParams(
            collective_id=0, has_side_effects=True, vmem_limit_bytes=56 * 1024 * 1024
        ),
        cost_estimate=pl.CostEstimate(
            flops=8_000_000_000, bytes_accessed=9_000_000, transcendentals=2_000_000
        ),
    )(
        tokens,
        grad_out,
        norm1_gain,
        qkv_weight,
        proj_weight,
        norm2_gain,
        up_weight,
        down_weight,
    )
    return pl.pallas_call(
        write_out,
        out_shape=(shape, shape),
        in_specs=[vmem_spec, vmem_spec],
        out_specs=(any_spec, any_spec),
        scratch_shapes=[pltpu.SemaphoreType.DMA((2, 3))],
        compiler_params=pltpu.CompilerParams(vmem_limit_bytes=8 * 1024 * 1024),
    )(*results)


def solution(mesh):
    grid = P("lon", "lat", None, None)
    return jax.shard_map(
        functools.partial(on_device, mesh.shape["lon"], mesh.shape["lat"]),
        mesh=mesh,
        in_specs=(grid, grid) + (P(),) * 6,
        out_specs=(grid, grid),
        check_vma=False,
    )
```

```python
import functools
import math

import jax
import jax.numpy as jnp
from jax import lax
from jax.experimental import pallas as pl
from jax.experimental.pallas import tpu as pltpu
from jax.sharding import PartitionSpec as P

MESH = pl.DeviceIdType.MESH
F32 = jnp.float32
BF16 = jnp.bfloat16
EPS = 1e-05
LON, LAT, LEV, D = 12, 6, 4, 512
POS = LON * LAT
ROWS = POS * LEV
WIN = ROWS // 2
FF = 2048
CHUNK = ROWS // 3
HALF_CHUNK = CHUNK // 2
PAIR = 128
HALF = 64


def dot(a, b):
    return jnp.dot(a, b, preferred_element_type=F32)


def dot_nt(a, b):
    return lax.dot_general(a, b, (((1,), (1,)), ((), ())), preferred_element_type=F32)


def norm_unit(x):
    centre = x - jnp.mean(x, -1, keepdims=True)
    inv_std = lax.rsqrt(jnp.mean(centre * centre, -1, keepdims=True) + EPS)
    return centre * inv_std, inv_std


def norm_grad(upstream, unit, inv_std, gain):
    scaled = upstream * gain
    return inv_std * (
        scaled
        - jnp.mean(scaled, -1, keepdims=True)
        - unit * jnp.mean(scaled * unit, -1, keepdims=True)
    )


def flat(ref):
    return ref[...].reshape(ROWS, D)


def natural_index(r, half):
    in_second = (r >= half).astype(jnp.int32)
    s = r - in_second * half
    odd = lax.rem(s, 2)
    level = jnp.where(in_second == 1, 3 - 3 * odd, 1 + odd)
    return (s // 2) * LEV + level


def kernel(
    nlon,
    nlat,
    tokens,
    grad_out,
    gain1_ref,
    wqkv_h,
    wproj_h,
    gain2_ref,
    wup_h,
    wdown_h,
    out_ref,
    tgrad_ref,
    wqkv,
    wproj,
    wup,
    wdown,
    perm,
    perm_back,
    perm_wide,
    bias,
    tok_b,
    gout_b,
    win_tok,
    att_res,
    att_b,
    ga_b,
    win_ga,
    gn_res,
    gn_b,
    qkv,
    k_t,
    v_t,
    turned,
    probs,
    gqkv,
    att,
    gh,
    act,
    gpre,
    mids,
    gmid,
    units,
    scales,
    wsem,
    lsem,
    ssem,
    rsem,
):
    lon = lax.axis_index("lon")
    lat = lax.axis_index("lat")
    east, west = lax.rem(lon + 1, nlon), lax.rem(lon + nlon - 1, nlon)
    north, south = lax.rem(lat + 1, nlat), lax.rem(lat + nlat - 1, nlat)

    def column(index):
        odd = lax.rem(index, 2)
        near, far = 3 * odd, 3 - 3 * odd
        return near, far, odd * south + (1 - odd) * north

    near, far, far_to = column(lon)
    near_e, far_e, far_to_e = column(east)
    far_from = north + south - far_to
    to_e, to_w = (east, lat), (west, lat)
    to_far, to_from = (lon, far_to), (lon, far_from)
    to_e_far, to_w_from = (east, far_to_e), (west, far_from)

    barrier = pltpu.get_barrier_semaphore()
    for device in (to_e, to_w, to_far, to_from, to_e_far, to_w_from):
        pl.semaphore_signal(barrier, inc=1, device_id=device, device_id_type=MESH)

    loads = []

    def load(src, dst, sem):
        copy = pltpu.make_async_copy(src, dst, sem)
        copy.start()
        return copy

    go_copies = [
        load(grad_out.at[:, 0:3], gout_b.at[0, :, 0:3], lsem.at[0]),
        load(grad_out.at[:, 9:12], gout_b.at[0, :, 3:6], lsem.at[1]),
        load(grad_out.at[:, 3:9], gout_b.at[1], lsem.at[2]),
    ]
    down_copy = load(wdown_h, wdown, wsem.at[0])
    own_copies = [
        load(tokens.at[0:6, pl.ds(3 * near, 3)], win_tok.at[0, 6:12, pl.ds(3 - near, 3)], lsem.at[3]),
        load(tokens.at[6:12, 3:9], win_tok.at[1, 0:6], lsem.at[4]),
    ]
    qkv_copy = load(wqkv_h, wqkv, wsem.at[1])
    tok_copies = [
        load(tokens.at[:, 0:3], tok_b.at[0, :, 0:3], lsem.at[5]),
        load(tokens.at[:, 9:12], tok_b.at[0, :, 3:6], lsem.at[6]),
        load(tokens.at[:, 3:9], tok_b.at[1], lsem.at[7]),
    ]
    proj_copy = load(wproj_h, wproj, wsem.at[2])
    up_copy = load(wup_h, wup, wsem.at[3])

    rows = lax.broadcasted_iota(jnp.int32, (CHUNK, CHUNK), 0)
    cols = lax.broadcasted_iota(jnp.int32, (CHUNK, CHUNK), 1)
    perm[...] = (natural_index(rows, HALF_CHUNK) == cols).astype(F32).astype(BF16)
    perm_back[...] = (natural_index(cols, HALF_CHUNK) == rows).astype(F32).astype(BF16)
    rows = lax.broadcasted_iota(jnp.int32, (ROWS, WIN), 0)
    cols = lax.broadcasted_iota(jnp.int32, (ROWS, WIN), 1)
    for window in range(2):
        perm_wide[window] = (natural_index(cols + window * WIN, WIN) == rows).astype(F32).astype(BF16)
    odd = lax.rem(lon, 2)
    edge = (lat == odd * (nlat - 1)).astype(jnp.int32)
    row = lax.broadcasted_iota(jnp.int32, (WIN, WIN), 0)
    col = lax.broadcasted_iota(jnp.int32, (WIN, WIN), 1)
    parity = (lax.rem(row, 2) != lax.rem(col, 2)).astype(jnp.int32)
    half_r = (lax.rem(row // 2, LAT) >= LAT // 2).astype(jnp.int32)
    half_c = (lax.rem(col // 2, LAT) >= LAT // 2).astype(jnp.int32)
    across = (half_r != half_c).astype(jnp.int32) * edge
    blocked = ((across, parity + across), (jnp.zeros_like(parity), parity))
    for group in range(2):
        for window in range(2):
            bias[group, window] = jnp.where(blocked[group][window] > 0, -1e30, 0.0)

    pl.semaphore_wait(barrier, 6)

    def send(phase, slot, src, dst, device):
        copy = pltpu.make_async_remote_copy(
            src_ref=src,
            dst_ref=dst,
            send_sem=ssem.at[phase, slot],
            recv_sem=rsem.at[phase, slot],
            device_id=device,
            device_id_type=MESH,
        )
        copy.start()
        return copy

    tok_sends_c = [
        send(0, 0, tokens.at[6:12, pl.ds(3 * far_e, 3)], win_tok.at[0, 0:6, pl.ds(3 - far_e, 3)], to_e_far),
        send(0, 1, tokens.at[0:6, pl.ds(3 * far, 3)], win_tok.at[0, 6:12, pl.ds(3 - far, 3)], to_far),
        send(0, 2, tokens.at[6:12, pl.ds(3 * near_e, 3)], win_tok.at[0, 0:6, pl.ds(3 - near_e, 3)], to_e),
    ]
    tok_sends_l = [send(0, 3, tokens.at[0:6, 3:9], win_tok.at[1, 6:12], to_w)]

    def inward(phase, block, src):
        if block == 0:
            return [
                send(phase, 0, src.at[0, 6:12, pl.ds(far_e, 3)], win_ga.at[0, 0:6, pl.ds(3 - far_e, 3)], to_e_far),
                send(phase, 1, src.at[0, 0:6, pl.ds(far, 3)], win_ga.at[0, 6:12, pl.ds(3 - far, 3)], to_far),
                send(phase, 2, src.at[0, 6:12, pl.ds(near_e, 3)], win_ga.at[0, 0:6, pl.ds(3 - near_e, 3)], to_e),
            ]
        return [send(phase, 3, src.at[1, 0:6], win_ga.at[1, 6:12], to_w)]

    def outward(phase, group, src, dst):
        if group == 0:
            return [
                send(phase, 0, src.at[0, 0:6, pl.ds(3 - far, 3)], dst.at[0, 6:12, pl.ds(far, 3)], to_w_from),
                send(phase, 1, src.at[0, 6:12, pl.ds(3 - far, 3)], dst.at[0, 0:6, pl.ds(far, 3)], to_from),
                send(phase, 2, src.at[0, 0:6, pl.ds(3 - near, 3)], dst.at[0, 6:12, pl.ds(near, 3)], to_w),
            ]
        return [send(phase, 3, src.at[1, 6:12], dst.at[1, 0:6], to_e)]

    def keep_outward(group, value, res, dst):
        if group == 0:
            dst[0, 0:6, pl.ds(near, 3)] = res[0, 6:12, pl.ds(3 - near, 3)]
        else:
            dst[1, 6:12] = value[0:6]

    low = lax.broadcasted_iota(jnp.int32, (WIN, PAIR), 1) < HALF
    gain1 = gain1_ref[...].astype(F32).reshape(1, D)
    gain2 = gain2_ref[...].astype(F32).reshape(1, D)

    def both(pair):
        zero = jnp.zeros_like(pair)
        return jnp.concatenate([jnp.where(low, pair, zero), jnp.where(low, zero, pair)], 0)

    for copy in go_copies:
        copy.wait()
    down_copy.wait()
    rows_out = gout_b[...].reshape(2 * ROWS, D)
    for part in range(4):
        span = slice(part * 512, part * 512 + 512)
        gh[:, :, span] = dot_nt(rows_out, wdown[span, :]).reshape(2, ROWS, 512)
    for copy in tok_copies:
        copy.wait()
    for block in range(2):
        units[block], scales[block] = norm_unit(tok_b[block].reshape(ROWS, D).astype(F32))
    for copy in own_copies:
        copy.wait()
    qkv_copy.wait()

    def to_windows(rows):
        parts = [dot(perm[...], rows[CHUNK * c : CHUNK * c + CHUNK]).astype(BF16) for c in range(3)]
        return jnp.concatenate([p[:HALF_CHUNK] for p in parts] + [p[HALF_CHUNK:] for p in parts], 0)

    def from_windows(rows):
        parts = []
        for c in range(3):
            first = rows[HALF_CHUNK * c : HALF_CHUNK * c + HALF_CHUNK]
            second = rows[WIN + HALF_CHUNK * c : WIN + HALF_CHUNK * c + HALF_CHUNK]
            parts.append(dot(perm_back[...], jnp.concatenate([first, second], 0)).astype(BF16))
        return jnp.concatenate(parts, 0)

    def forward(group, arrivals):
        for copy in arrivals:
            copy.wait_recv()
        unit, _ = norm_unit(win_tok[group].reshape(ROWS, D).astype(F32))
        normed = to_windows((unit * gain1).astype(BF16))
        q = dot(normed, wqkv[:, 0:D]).astype(BF16)
        qkv[group, :, 0:D] = q * jnp.asarray(0.125, BF16)
        k = dot(normed, wqkv[:, D : 2 * D]).astype(BF16)
        qkv[group, :, D : 2 * D] = k
        v = dot(normed, wqkv[:, 2 * D : 3 * D]).astype(BF16)
        qkv[group, :, 2 * D : 3 * D] = v
        for window in range(2):
            span = slice(window * WIN, window * WIN + WIN)
            k_t[group, window] = k[span].T
            v_t[window] = v[span].T

        spans = [slice(window * WIN, window * WIN + WIN) for window in range(2)]
        scores = {}
        for window in range(2):
            for pair in range(4):
                q_pair = qkv[group, spans[window], pair * PAIR : pair * PAIR + PAIR]
                k_pair = qkv[group, spans[window], D + pair * PAIR : D + pair * PAIR + PAIR]
                scores[window, pair] = dot_nt(both(k_pair), q_pair)
        weights = {}
        for window in range(2):
            for head in range(8):
                row = head % 2 * WIN
                score = scores[window, head // 2][row : row + WIN] + bias[group, window]
                expo = jnp.exp(score - jnp.max(score, 0, keepdims=True))
                prob = (expo * (1.0 / jnp.sum(expo, 0, keepdims=True))).astype(BF16)
                probs[group, window, head] = prob
                weights[window, head] = prob
        for window in range(2):
            for head in range(8):
                lanes = slice(head * HALF, head * HALF + HALF)
                turned[window, lanes] = dot(v_t[window, lanes], weights[window, head]).astype(BF16)
        result = dot_nt(perm_wide[0], turned[0]) + dot_nt(perm_wide[1], turned[1])
        result = result.astype(BF16).reshape(LON, LAT, LEV, D)
        att_res[group] = result
        keep_outward(group, result, att_res, att_b)
        return outward(1, group, att_res, att_b)

    def tail(block, arrivals):
        for copy in arrivals:
            copy.wait_recv()
        mixed = dot(att_b[block].reshape(ROWS, D), wproj[...])
        mid = (tok_b[block].reshape(ROWS, D).astype(F32) + mixed).astype(BF16)
        mids[block] = mid
        unit, inv_std = norm_unit(mid.astype(F32))
        normed = (unit * gain2).astype(BF16)
        for part in range(4):
            span = slice(part * 512, part * 512 + 512)
            x = dot(normed, wup[:, span])
            c = math.sqrt(2.0 / math.pi)
            square = x * x
            cdf = 0.5 + 0.5 * jnp.tanh(x * (c + (c * 0.044715) * square))
            active = x * cdf
            act[block, :, span] = active.astype(BF16)
            slope = cdf * (1.0 + (x - active) * (2.0 * c + (6.0 * c * 0.044715) * square))
            gpre[:, span] = (slope * gh[block, :, span]).astype(BF16)
        grad_normed = dot_nt(gpre[...], wup[...])
        grad_rows = gout_b[block].reshape(ROWS, D).astype(F32)
        grad_mid = (grad_rows + norm_grad(grad_normed, unit, inv_std, gain2)).astype(BF16)
        gmid[block] = grad_mid
        grad_att = dot_nt(grad_mid, wproj[...]).astype(BF16).reshape(LON, LAT, LEV, D)
        ga_b[block] = grad_att
        sends = inward(2, block, ga_b)
        if block == 0:
            win_ga[0, 6:12, pl.ds(3 - near, 3)] = ga_b[0, 0:6, pl.ds(near, 3)]
        else:
            win_ga[1, 0:6] = grad_att[6:12]
        return sends

    def lower(block):
        output = (mids[block].astype(F32) + dot(act[block], wdown[...])).astype(BF16)
        store(block, output.reshape(LON, LAT, LEV, D), out_ref)

    def store(block, value, dst):
        if block == 0:
            dst[:, 0:3] = value[:, 0:3]
            dst[:, 9:12] = value[:, 3:6]
        else:
            dst[:, 3:9] = value

    def backward(group, arrivals):
        for copy in arrivals:
            copy.wait_recv()
        att[...] = to_windows(win_ga[group].reshape(ROWS, D))

        spans = [slice(window * WIN, window * WIN + WIN) for window in range(2)]
        lanes = [slice(pair * PAIR, pair * PAIR + PAIR) for pair in range(4)]
        k_lanes = [slice(D + pair * PAIR, D + pair * PAIR + PAIR) for pair in range(4)]
        v_lanes = [slice(2 * D + pair * PAIR, 2 * D + pair * PAIR + PAIR) for pair in range(4)]
        grad_probs = {}
        for window in range(2):
            for pair in range(4):
                v_pair = qkv[group, spans[window], v_lanes[pair]]
                grad_probs[window, pair] = dot_nt(both(v_pair), att[spans[window], lanes[pair]])
        for window in range(2):
            for pair in range(4):
                prob = probs[group, window, 2 * pair : 2 * pair + 2].reshape(2 * WIN, WIN)
                grad_v = dot(prob, att[spans[window], lanes[pair]])
                gqkv[spans[window], v_lanes[pair]] = jnp.where(low, grad_v[:WIN], grad_v[WIN:]).astype(BF16)
        grad_scores = {}
        for window in range(2):
            for head in range(8):
                row = head % 2 * WIN
                wide = probs[group, window, head].astype(F32)
                grad_prob = grad_probs[window, head // 2][row : row + WIN]
                total = jnp.sum(grad_prob * wide, 0, keepdims=True)
                grad_scores[window, head] = (wide * (grad_prob - total)).astype(BF16)
        for window in range(2):
            for head in range(8):
                turned_rows = slice(head * HALF, head * HALF + HALF)
                grad_q = dot(k_t[group, window, turned_rows], grad_scores[window, head])
                turned[window, turned_rows] = (grad_q * 0.125).astype(BF16)
        for window in range(2):
            for pair in range(4):
                grad_score = jnp.concatenate([grad_scores[window, 2 * pair + h] for h in range(2)], 0)
                grad_k = dot(grad_score, qkv[group, spans[window], lanes[pair]])
                gqkv[spans[window], k_lanes[pair]] = jnp.where(low, grad_k[:WIN], grad_k[WIN:]).astype(BF16)
        for window in range(2):
            gqkv[window * WIN : window * WIN + WIN, 0:D] = turned[window].T
        result = from_windows(dot_nt(gqkv[...], wqkv[...]).astype(BF16)).reshape(LON, LAT, LEV, D)
        gn_res[group] = result
        keep_outward(group, result, gn_res, gn_b)
        return outward(3, group, gn_res, gn_b)

    def finish(block, arrivals):
        for copy in arrivals:
            copy.wait_recv()
        upstream = gn_b[block].reshape(ROWS, D).astype(F32)
        total = gmid[block].astype(F32) + norm_grad(upstream, units[block], scales[block], gain1)
        store(block, total.astype(BF16).reshape(LON, LAT, LEV, D), tgrad_ref)

    att_sends_c = forward(0, tok_sends_c)
    att_sends_l = forward(1, tok_sends_l)
    proj_copy.wait()
    up_copy.wait()
    ga_sends_c = tail(0, att_sends_c)
    ga_sends_l = tail(1, att_sends_l)
    lower(0)
    gn_sends_c = backward(0, ga_sends_c)
    gn_sends_l = backward(1, ga_sends_l)
    lower(1)
    finish(0, gn_sends_c)
    finish(1, gn_sends_l)
    for copy in tok_sends_c + tok_sends_l + att_sends_c + att_sends_l:
        copy.wait_send()
    for copy in ga_sends_c + ga_sends_l + gn_sends_c + gn_sends_l:
        copy.wait_send()


def write_out(out_ref, tgrad_ref, out_h, tgrad_h, sem):
    copies = []
    for which, (src, dst) in enumerate(((out_ref, out_h), (tgrad_ref, tgrad_h))):
        for part in range(3):
            span = slice(4 * part, 4 * part + 4)
            copies.append(pltpu.make_async_copy(src.at[span], dst.at[span], sem.at[which, part]))
    for copy in copies:
        copy.start()
    for copy in copies:
        copy.wait()


def on_device(
    nlon,
    nlat,
    tokens,
    grad_out,
    norm1_gain,
    qkv_weight,
    proj_weight,
    norm2_gain,
    up_weight,
    down_weight,
):
    any_spec = pl.BlockSpec(memory_space=pl.ANY)
    vmem_spec = pl.BlockSpec(memory_space=pltpu.VMEM)
    shape = jax.ShapeDtypeStruct(tokens.shape, BF16)
    block = (2, LON, LAT, LEV, D)
    in_vmem = pltpu.VMEM(tokens.shape, BF16)
    results = pl.pallas_call(
        functools.partial(kernel, nlon, nlat),
        out_shape=(in_vmem, in_vmem),
        in_specs=[any_spec, any_spec, vmem_spec, any_spec, any_spec, vmem_spec, any_spec, any_spec],
        out_specs=(vmem_spec, vmem_spec),
        scratch_shapes=[
            pltpu.VMEM((D, 3 * D), BF16),
            pltpu.VMEM((D, D), BF16),
            pltpu.VMEM((D, FF), BF16),
            pltpu.VMEM((FF, D), BF16),
            pltpu.VMEM((CHUNK, CHUNK), BF16),
            pltpu.VMEM((CHUNK, CHUNK), BF16),
            pltpu.VMEM((2, ROWS, WIN), BF16),
            pltpu.VMEM((2, 2, WIN, WIN), F32),
            pltpu.VMEM(block, BF16),
            pltpu.VMEM(block, BF16),
            pltpu.VMEM(block, BF16),
            pltpu.VMEM(block, BF16),
            pltpu.VMEM(block, BF16),
            pltpu.VMEM(block, BF16),
            pltpu.VMEM(block, BF16),
            pltpu.VMEM(block, BF16),
            pltpu.VMEM(block, BF16),
            pltpu.VMEM((2, ROWS, 3 * D), BF16),
            pltpu.VMEM((2, 2, D, WIN), BF16),
            pltpu.VMEM((2, D, WIN), BF16),
            pltpu.VMEM((2, D, WIN), BF16),
            pltpu.VMEM((2, 2, 8, WIN, WIN), BF16),
            pltpu.VMEM((ROWS, 3 * D), BF16),
            pltpu.VMEM((ROWS, D), BF16),
            pltpu.VMEM((2, ROWS, FF), F32),
            pltpu.VMEM((2, ROWS, FF), BF16),
            pltpu.VMEM((ROWS, FF), BF16),
            pltpu.VMEM((2, ROWS, D), BF16),
            pltpu.VMEM((2, ROWS, D), BF16),
            pltpu.VMEM((2, ROWS, D), F32),
            pltpu.VMEM((2, ROWS, 1), F32),
            pltpu.SemaphoreType.DMA((4,)),
            pltpu.SemaphoreType.DMA((8,)),
            pltpu.SemaphoreType.DMA((4, 4)),
            pltpu.SemaphoreType.DMA((4, 4)),
        ],
        compiler_params=pltpu.CompilerParams(
            collective_id=0, has_side_effects=True, vmem_limit_bytes=56 * 1024 * 1024
        ),
        cost_estimate=pl.CostEstimate(
            flops=8_000_000_000, bytes_accessed=9_000_000, transcendentals=2_000_000
        ),
    )(
        tokens,
        grad_out,
        norm1_gain,
        qkv_weight,
        proj_weight,
        norm2_gain,
        up_weight,
        down_weight,
    )
    return pl.pallas_call(
        write_out,
        out_shape=(shape, shape),
        in_specs=[vmem_spec, vmem_spec],
        out_specs=(any_spec, any_spec),
        scratch_shapes=[pltpu.SemaphoreType.DMA((2, 3))],
        compiler_params=pltpu.CompilerParams(vmem_limit_bytes=8 * 1024 * 1024),
    )(*results)


def solution(mesh):
    grid = P("lon", "lat", None, None)
    return jax.shard_map(
        functools.partial(on_device, mesh.shape["lon"], mesh.shape["lat"]),
        mesh=mesh,
        in_specs=(grid, grid) + (P(),) * 6,
        out_specs=(grid, grid),
        check_vma=False,
    )
```

```python
import functools
import math

import jax
import jax.numpy as jnp
from jax import lax
from jax.experimental import pallas as pl
from jax.experimental.pallas import tpu as pltpu
from jax.sharding import PartitionSpec as P

MESH = pl.DeviceIdType.MESH
F32 = jnp.float32
BF16 = jnp.bfloat16
EPS = 1e-05
LON, LAT, LEV, D = 12, 6, 4, 512
POS = LON * LAT
ROWS = POS * LEV
WIN = ROWS // 2
FF = 2048
CHUNK = ROWS // 3
HALF_CHUNK = CHUNK // 2
PAIR = 128
ORDER = (1, 0)
HALF = 64


def dot(a, b):
    return jnp.dot(a, b, preferred_element_type=F32)


def dot_nt(a, b):
    return lax.dot_general(a, b, (((1,), (1,)), ((), ())), preferred_element_type=F32)


def norm_unit(x):
    centre = x - jnp.mean(x, -1, keepdims=True)
    inv_std = lax.rsqrt(jnp.mean(centre * centre, -1, keepdims=True) + EPS)
    return centre * inv_std, inv_std


def norm_grad(upstream, unit, inv_std, gain):
    scaled = upstream * gain
    return inv_std * (
        scaled
        - jnp.mean(scaled, -1, keepdims=True)
        - unit * jnp.mean(scaled * unit, -1, keepdims=True)
    )


def natural_index(r, half):
    in_second = (r >= half).astype(jnp.int32)
    s = r - in_second * half
    odd = lax.rem(s, 2)
    level = jnp.where(in_second == 1, 3 - 3 * odd, 1 + odd)
    return (s // 2) * LEV + level


def kernel(
    nlon,
    nlat,
    tokens,
    grad_out,
    gain1_ref,
    wqkv_h,
    wproj_h,
    gain2_ref,
    wup_h,
    wdown_h,
    out_ref,
    tgrad_ref,
    wqkv,
    wproj,
    wup,
    wdown,
    perm,
    perm_back,
    bias,
    win_tok,
    win_go,
    out_res,
    tgrad_res,
    qkv,
    k_t,
    v_t,
    turned,
    probs,
    gqkv,
    att,
    act,
    gpre,
    rows_in,
    units,
    scales,
    wsem,
    lsem,
    ssem,
    rsem,
):
    lon = lax.axis_index("lon")
    lat = lax.axis_index("lat")
    east, west = lax.rem(lon + 1, nlon), lax.rem(lon + nlon - 1, nlon)
    north, south = lax.rem(lat + 1, nlat), lax.rem(lat + nlat - 1, nlat)

    def column(index):
        odd = lax.rem(index, 2)
        near, far = 3 * odd, 3 - 3 * odd
        return near, far, odd * south + (1 - odd) * north

    near, far, far_to = column(lon)
    near_e, far_e, far_to_e = column(east)
    far_from = north + south - far_to
    to_e, to_w = (east, lat), (west, lat)
    to_far, to_from = (lon, far_to), (lon, far_from)
    to_e_far, to_w_from = (east, far_to_e), (west, far_from)

    barrier = pltpu.get_barrier_semaphore()
    for device in (to_e, to_w, to_far, to_from, to_e_far, to_w_from):
        pl.semaphore_signal(barrier, inc=1, device_id=device, device_id_type=MESH)

    def load(src, dst, sem):
        copy = pltpu.make_async_copy(src, dst, sem)
        copy.start()
        return copy

    def load_own(group, src, dst, sem):
        if group == 0:
            return load(src.at[0:6, pl.ds(3 * near, 3)], dst.at[0, 6:12, pl.ds(3 - near, 3)], sem)
        return load(src.at[6:12, 3:9], dst.at[1, 0:6], sem)

    own_tok = {group: load_own(group, tokens, win_tok, lsem.at[group]) for group in ORDER}
    qkv_copy = load(wqkv_h, wqkv, wsem.at[0])
    own_go = {group: load_own(group, grad_out, win_go, lsem.at[2 + group]) for group in ORDER}
    tail_copies = [
        load(wproj_h, wproj, wsem.at[1]),
        load(wup_h, wup, wsem.at[2]),
        load(wdown_h, wdown, wsem.at[3]),
    ]

    rows = lax.broadcasted_iota(jnp.int32, (CHUNK, CHUNK), 0)
    cols = lax.broadcasted_iota(jnp.int32, (CHUNK, CHUNK), 1)
    perm[...] = (natural_index(rows, HALF_CHUNK) == cols).astype(F32).astype(BF16)
    perm_back[...] = (natural_index(cols, HALF_CHUNK) == rows).astype(F32).astype(BF16)
    odd = lax.rem(lon, 2)
    edge = (lat == odd * (nlat - 1)).astype(jnp.int32)
    row = lax.broadcasted_iota(jnp.int32, (WIN, WIN), 0)
    col = lax.broadcasted_iota(jnp.int32, (WIN, WIN), 1)
    parity = (lax.rem(row, 2) != lax.rem(col, 2)).astype(jnp.int32)
    half_r = (lax.rem(row // 2, LAT) >= LAT // 2).astype(jnp.int32)
    half_c = (lax.rem(col // 2, LAT) >= LAT // 2).astype(jnp.int32)
    across = (half_r != half_c).astype(jnp.int32) * edge
    blocked = ((across, parity + across), (jnp.zeros_like(parity), parity))
    for group in range(2):
        for window in range(2):
            bias[group, window] = jnp.where(blocked[group][window] > 0, -1e30, 0.0)

    pl.semaphore_wait(barrier, 6)

    def send(phase, slot, src, dst, device):
        copy = pltpu.make_async_remote_copy(
            src_ref=src,
            dst_ref=dst,
            send_sem=ssem.at[phase, slot],
            recv_sem=rsem.at[phase, slot],
            device_id=device,
            device_id_type=MESH,
        )
        copy.start()
        return copy

    def inward(phase, group, src, dst):
        if group == 0:
            return [
                send(phase, 0, src.at[6:12, pl.ds(3 * far_e, 3)], dst.at[0, 0:6, pl.ds(3 - far_e, 3)], to_e_far),
                send(phase, 1, src.at[0:6, pl.ds(3 * far, 3)], dst.at[0, 6:12, pl.ds(3 - far, 3)], to_far),
                send(phase, 2, src.at[6:12, pl.ds(3 * near_e, 3)], dst.at[0, 0:6, pl.ds(3 - near_e, 3)], to_e),
            ]
        return [send(phase, 3, src.at[0:6, 3:9], dst.at[1, 6:12], to_w)]

    def outward(phase, group, value, res, dst):
        res[group] = value
        if group == 0:
            sends = [
                send(phase, 0, res.at[0, 0:6, pl.ds(3 - far, 3)], dst.at[6:12, pl.ds(3 * far, 3)], to_w_from),
                send(phase, 1, res.at[0, 6:12, pl.ds(3 - far, 3)], dst.at[0:6, pl.ds(3 * far, 3)], to_from),
                send(phase, 2, res.at[0, 0:6, pl.ds(3 - near, 3)], dst.at[6:12, pl.ds(3 * near, 3)], to_w),
            ]
            dst[0:6, pl.ds(3 * near, 3)] = res[0, 6:12, pl.ds(3 - near, 3)]
        else:
            sends = [send(phase, 3, res.at[1, 6:12], dst.at[0:6, 3:9], to_e)]
            dst[6:12, 3:9] = value[0:6]
        return sends

    tok_sends = {group: inward(0, group, tokens, win_tok) for group in ORDER}
    go_sends = {group: inward(1, group, grad_out, win_go) for group in ORDER}

    low = lax.broadcasted_iota(jnp.int32, (WIN, PAIR), 1) < HALF
    gain1 = gain1_ref[...].astype(F32).reshape(1, D)
    gain2 = gain2_ref[...].astype(F32).reshape(1, D)

    def both(pair):
        zero = jnp.zeros_like(pair)
        return jnp.concatenate([jnp.where(low, pair, zero), jnp.where(low, zero, pair)], 0)

    def to_windows(rows):
        parts = [dot(perm[...], rows[CHUNK * c : CHUNK * c + CHUNK]).astype(BF16) for c in range(3)]
        return jnp.concatenate([p[:HALF_CHUNK] for p in parts] + [p[HALF_CHUNK:] for p in parts], 0)

    def from_windows(rows):
        parts = []
        for c in range(3):
            first = rows[HALF_CHUNK * c : HALF_CHUNK * c + HALF_CHUNK]
            second = rows[WIN + HALF_CHUNK * c : WIN + HALF_CHUNK * c + HALF_CHUNK]
            parts.append(dot(perm_back[...], jnp.concatenate([first, second], 0)).astype(BF16))
        return jnp.concatenate(parts, 0)

    def forward(group):
        own_tok[group].wait()
        for copy in tok_sends[group]:
            copy.wait_recv()
        rows = to_windows(win_tok[group].reshape(ROWS, D))
        rows_in[...] = rows
        unit, scales[...] = norm_unit(rows.astype(F32))
        units[...] = unit
        normed = (unit * gain1).astype(BF16)
        if group == ORDER[0]:
            qkv_copy.wait()
        q = dot(normed, wqkv[:, 0:D]).astype(BF16)
        qkv[:, 0:D] = q * jnp.asarray(0.125, BF16)
        qkv[:, D : 2 * D] = dot(normed, wqkv[:, D : 2 * D]).astype(BF16)
        v = dot(normed, wqkv[:, 2 * D : 3 * D]).astype(BF16)
        qkv[:, 2 * D : 3 * D] = v
        for window in range(2):
            span = slice(window * WIN, window * WIN + WIN)
            v_t[window] = v[span].T

        spans = [slice(window * WIN, window * WIN + WIN) for window in range(2)]
        scores = {}
        for window in range(2):
            for pair in range(4):
                q_pair = qkv[spans[window], pair * PAIR : pair * PAIR + PAIR]
                k_pair = qkv[spans[window], D + pair * PAIR : D + pair * PAIR + PAIR]
                scores[window, pair] = dot_nt(both(k_pair), q_pair)
        weights = {}
        for window in range(2):
            for head in range(8):
                row = head % 2 * WIN
                score = scores[window, head // 2][row : row + WIN] + bias[group, window]
                expo = jnp.exp(score - jnp.max(score, 0, keepdims=True))
                prob = (expo * (1.0 / jnp.sum(expo, 0, keepdims=True))).astype(BF16)
                probs[window, head] = prob
                weights[window, head] = prob
        for window in range(2):
            for head in range(8):
                lanes = slice(head * HALF, head * HALF + HALF)
                turned[window, lanes] = dot(v_t[window, lanes], weights[window, head]).astype(BF16)
        return jnp.concatenate([turned[window].T for window in range(2)], 0)

    def tail(group, attended):
        if group == ORDER[0]:
            for copy in tail_copies:
                copy.wait()
        mid = (rows_in[...].astype(F32) + dot(attended, wproj[...])).astype(BF16)
        unit, inv_std = norm_unit(mid.astype(F32))
        normed = (unit * gain2).astype(BF16)
        own_go[group].wait()
        for copy in go_sends[group]:
            copy.wait_recv()
        grad_rows = to_windows(win_go[group].reshape(ROWS, D))
        for part in range(4):
            span = slice(part * 512, part * 512 + 512)
            grad_hidden = dot_nt(grad_rows, wdown[span, :])
            x = dot(normed, wup[:, span])
            c = math.sqrt(2.0 / math.pi)
            square = x * x
            cdf = 0.5 + 0.5 * jnp.tanh(x * (c + (c * 0.044715) * square))
            active = x * cdf
            act[:, span] = active.astype(BF16)
            slope = cdf * (1.0 + (x - active) * (2.0 * c + (6.0 * c * 0.044715) * square))
            gpre[:, span] = (slope * grad_hidden).astype(BF16)
        output = (mid.astype(F32) + dot(act[...], wdown[...])).astype(BF16)
        sends = outward(2, group, from_windows(output).reshape(LON, LAT, LEV, D), out_res, out_ref)
        grad_normed = dot_nt(gpre[...], wup[...])
        grad_mid = (grad_rows.astype(F32) + norm_grad(grad_normed, unit, inv_std, gain2)).astype(BF16)
        att[...] = dot_nt(grad_mid, wproj[...]).astype(BF16)
        return grad_mid, sends

    def backward(group, grad_mid):
        for window in range(2):
            k_t[window] = qkv[window * WIN : window * WIN + WIN, D : 2 * D].T
        spans = [slice(window * WIN, window * WIN + WIN) for window in range(2)]
        lanes = [slice(pair * PAIR, pair * PAIR + PAIR) for pair in range(4)]
        k_lanes = [slice(D + pair * PAIR, D + pair * PAIR + PAIR) for pair in range(4)]
        v_lanes = [slice(2 * D + pair * PAIR, 2 * D + pair * PAIR + PAIR) for pair in range(4)]
        grad_probs = {}
        for window in range(2):
            for pair in range(4):
                v_pair = qkv[spans[window], v_lanes[pair]]
                grad_probs[window, pair] = dot_nt(both(v_pair), att[spans[window], lanes[pair]])
        for window in range(2):
            for pair in range(4):
                prob = probs[window, 2 * pair : 2 * pair + 2].reshape(2 * WIN, WIN)
                grad_v = dot(prob, att[spans[window], lanes[pair]])
                gqkv[spans[window], v_lanes[pair]] = jnp.where(low, grad_v[:WIN], grad_v[WIN:]).astype(BF16)
        grad_scores = {}
        for window in range(2):
            for head in range(8):
                row = head % 2 * WIN
                wide = probs[window, head].astype(F32)
                grad_prob = grad_probs[window, head // 2][row : row + WIN]
                total = jnp.sum(grad_prob * wide, 0, keepdims=True)
                grad_scores[window, head] = (wide * (grad_prob - total)).astype(BF16)
        for window in range(2):
            for head in range(8):
                turned_rows = slice(head * HALF, head * HALF + HALF)
                grad_q = dot(k_t[window, turned_rows], grad_scores[window, head])
                turned[window, turned_rows] = (grad_q * 0.125).astype(BF16)
        for window in range(2):
            for pair in range(4):
                grad_score = jnp.concatenate([grad_scores[window, 2 * pair + h] for h in range(2)], 0)
                grad_k = dot(grad_score, qkv[spans[window], lanes[pair]])
                gqkv[spans[window], k_lanes[pair]] = jnp.where(low, grad_k[:WIN], grad_k[WIN:]).astype(BF16)
        for window in range(2):
            gqkv[window * WIN : window * WIN + WIN, 0:D] = turned[window].T
        grad_normed = dot_nt(gqkv[...], wqkv[...])
        total = grad_mid.astype(F32) + norm_grad(grad_normed, units[...], scales[...], gain1)
        result = from_windows(total.astype(BF16)).reshape(LON, LAT, LEV, D)
        return outward(3, group, result, tgrad_res, tgrad_ref)

    result_sends = []
    for group in ORDER:
        grad_mid, sends = tail(group, forward(group))
        result_sends += sends + backward(group, grad_mid)
    for copy in tok_sends[0] + tok_sends[1] + go_sends[0] + go_sends[1]:
        copy.wait_send()
    for copy in result_sends:
        copy.wait()


def write_out(out_ref, tgrad_ref, out_h, tgrad_h, sem):
    copies = []
    for which, (src, dst) in enumerate(((out_ref, out_h), (tgrad_ref, tgrad_h))):
        for part in range(3):
            span = slice(4 * part, 4 * part + 4)
            copies.append(pltpu.make_async_copy(src.at[span], dst.at[span], sem.at[which, part]))
    for copy in copies:
        copy.start()
    for copy in copies:
        copy.wait()


def on_device(
    nlon,
    nlat,
    tokens,
    grad_out,
    norm1_gain,
    qkv_weight,
    proj_weight,
    norm2_gain,
    up_weight,
    down_weight,
):
    any_spec = pl.BlockSpec(memory_space=pl.ANY)
    vmem_spec = pl.BlockSpec(memory_space=pltpu.VMEM)
    shape = jax.ShapeDtypeStruct(tokens.shape, BF16)
    block = (2, LON, LAT, LEV, D)
    in_vmem = pltpu.VMEM(tokens.shape, BF16)
    results = pl.pallas_call(
        functools.partial(kernel, nlon, nlat),
        out_shape=(in_vmem, in_vmem),
        in_specs=[any_spec, any_spec, vmem_spec, any_spec, any_spec, vmem_spec, any_spec, any_spec],
        out_specs=(vmem_spec, vmem_spec),
        scratch_shapes=[
            pltpu.VMEM((D, 3 * D), BF16),
            pltpu.VMEM((D, D), BF16),
            pltpu.VMEM((D, FF), BF16),
            pltpu.VMEM((FF, D), BF16),
            pltpu.VMEM((CHUNK, CHUNK), BF16),
            pltpu.VMEM((CHUNK, CHUNK), BF16),
            pltpu.VMEM((2, 2, WIN, WIN), F32),
            pltpu.VMEM(block, BF16),
            pltpu.VMEM(block, BF16),
            pltpu.VMEM(block, BF16),
            pltpu.VMEM(block, BF16),
            pltpu.VMEM((ROWS, 3 * D), BF16),
            pltpu.VMEM((2, D, WIN), BF16),
            pltpu.VMEM((2, D, WIN), BF16),
            pltpu.VMEM((2, D, WIN), BF16),
            pltpu.VMEM((2, 8, WIN, WIN), BF16),
            pltpu.VMEM((ROWS, 3 * D), BF16),
            pltpu.VMEM((ROWS, D), BF16),
            pltpu.VMEM((ROWS, FF), BF16),
            pltpu.VMEM((ROWS, FF), BF16),
            pltpu.VMEM((ROWS, D), BF16),
            pltpu.VMEM((ROWS, D), F32),
            pltpu.VMEM((ROWS, 1), F32),
            pltpu.SemaphoreType.DMA((4,)),
            pltpu.SemaphoreType.DMA((4,)),
            pltpu.SemaphoreType.DMA((4, 4)),
            pltpu.SemaphoreType.DMA((4, 4)),
        ],
        compiler_params=pltpu.CompilerParams(
            collective_id=0, has_side_effects=True, vmem_limit_bytes=56 * 1024 * 1024
        ),
        cost_estimate=pl.CostEstimate(
            flops=8_000_000_000, bytes_accessed=9_000_000, transcendentals=2_000_000
        ),
    )(
        tokens,
        grad_out,
        norm1_gain,
        qkv_weight,
        proj_weight,
        norm2_gain,
        up_weight,
        down_weight,
    )
    return pl.pallas_call(
        write_out,
        out_shape=(shape, shape),
        in_specs=[vmem_spec, vmem_spec],
        out_specs=(any_spec, any_spec),
        scratch_shapes=[pltpu.SemaphoreType.DMA((2, 3))],
        compiler_params=pltpu.CompilerParams(vmem_limit_bytes=8 * 1024 * 1024),
    )(*results)


def solution(mesh):
    grid = P("lon", "lat", None, None)
    return jax.shard_map(
        functools.partial(on_device, mesh.shape["lon"], mesh.shape["lat"]),
        mesh=mesh,
        in_specs=(grid, grid) + (P(),) * 6,
        out_specs=(grid, grid),
        check_vma=False,
    )
```

```python
import functools
import math

import jax
import jax.numpy as jnp
from jax import lax
from jax.experimental import pallas as pl
from jax.experimental.pallas import tpu as pltpu
from jax.sharding import PartitionSpec as P

MESH = pl.DeviceIdType.MESH
F32 = jnp.float32
BF16 = jnp.bfloat16
EPS = 1e-05
LON, LAT, LEV, D = 12, 6, 4, 512
POS = LON * LAT
ROWS = POS * LEV
WIN = ROWS // 2
FF = 2048
LEVEL_ORDER = (1, 2, 3, 0)
PAIR = 128
TILES = D // PAIR
ORDER = (1, 0)
HALF = 64


def dot(a, b):
    return jnp.dot(a, b, preferred_element_type=F32)


def dot_nt(a, b):
    return lax.dot_general(a, b, (((1,), (1,)), ((), ())), preferred_element_type=F32)


def norm_unit(x):
    centre = x - jnp.mean(x, -1, keepdims=True)
    inv_std = lax.rsqrt(jnp.mean(centre * centre, -1, keepdims=True) + EPS)
    return centre * inv_std, inv_std


def norm_grad(upstream, unit, inv_std, gain):
    scaled = upstream * gain
    return inv_std * (
        scaled
        - jnp.mean(scaled, -1, keepdims=True)
        - unit * jnp.mean(scaled * unit, -1, keepdims=True)
    )


def kernel(
    nlon,
    nlat,
    tokens,
    grad_out,
    gain1_ref,
    wqkv_h,
    wproj_h,
    gain2_ref,
    wup_h,
    wdown_h,
    out_ref,
    tgrad_ref,
    wqkv,
    wproj,
    wup,
    wdown,
    bias,
    win_tok,
    win_go,
    out_res,
    tgrad_res,
    qkv,
    k_t,
    v_t,
    turned,
    probs,
    gqkv,
    att,
    act,
    gpre,
    gmid,
    rows_in,
    units,
    scales,
    grid_tok,
    grid_go,
    grid_out,
    grid_tgrad,
    wsem,
    lsem,
    ssem,
    rsem,
):
    lon = lax.axis_index("lon")
    lat = lax.axis_index("lat")
    east, west = lax.rem(lon + 1, nlon), lax.rem(lon + nlon - 1, nlon)
    north, south = lax.rem(lat + 1, nlat), lax.rem(lat + nlat - 1, nlat)

    def column(index):
        odd = lax.rem(index, 2)
        near, far = 3 * odd, 3 - 3 * odd
        return near, far, odd * south + (1 - odd) * north

    near, far, far_to = column(lon)
    near_e, far_e, far_to_e = column(east)
    far_from = north + south - far_to
    to_e, to_w = (east, lat), (west, lat)
    to_far, to_from = (lon, far_to), (lon, far_from)
    to_e_far, to_w_from = (east, far_to_e), (west, far_from)

    barrier = pltpu.get_barrier_semaphore()
    for device in (to_e, to_w, to_far, to_from, to_e_far, to_w_from):
        pl.semaphore_signal(barrier, inc=1, device_id=device, device_id_type=MESH)

    def load(src, dst, sem):
        copy = pltpu.make_async_copy(src, dst, sem)
        copy.start()
        return copy

    def load_own(group, src, dst, sem):
        if group == 0:
            return load(src.at[0:6, pl.ds(3 * near, 3)], dst.at[0, 6:12, pl.ds(3 - near, 3)], sem)
        return load(src.at[6:12, 3:9], dst.at[1, 0:6], sem)

    own_tok = {group: load_own(group, tokens, win_tok, lsem.at[group]) for group in ORDER}
    qkv_copy = load(wqkv_h, wqkv, wsem.at[0])
    own_go = {group: load_own(group, grad_out, win_go, lsem.at[2 + group]) for group in ORDER}
    tail_copies = [
        load(wproj_h, wproj, wsem.at[1]),
        load(wup_h, wup, wsem.at[2]),
        load(wdown_h, wdown, wsem.at[3]),
    ]

    odd = lax.rem(lon, 2)
    edge = (lat == odd * (nlat - 1)).astype(jnp.int32)
    row = lax.broadcasted_iota(jnp.int32, (WIN, WIN), 0)
    col = lax.broadcasted_iota(jnp.int32, (WIN, WIN), 1)
    levels = ((row >= POS) != (col >= POS)).astype(jnp.int32)
    half_r = (lax.rem(row, LAT) >= LAT // 2).astype(jnp.int32)
    half_c = (lax.rem(col, LAT) >= LAT // 2).astype(jnp.int32)
    across = (half_r != half_c).astype(jnp.int32) * edge
    blocked = ((across, levels + across), (jnp.zeros_like(levels), levels))
    for group in range(2):
        for window in range(2):
            bias[group, window] = jnp.where(blocked[group][window] > 0, -1e30, 0.0)

    pl.semaphore_wait(barrier, 6)

    def send(phase, slot, src, dst, device):
        copy = pltpu.make_async_remote_copy(
            src_ref=src,
            dst_ref=dst,
            send_sem=ssem.at[phase, slot],
            recv_sem=rsem.at[phase, slot],
            device_id=device,
            device_id_type=MESH,
        )
        copy.start()
        return copy

    def inward(phase, group, src, dst):
        if group == 0:
            return [
                send(phase, 0, src.at[6:12, pl.ds(3 * far_e, 3)], dst.at[0, 0:6, pl.ds(3 - far_e, 3)], to_e_far),
                send(phase, 1, src.at[0:6, pl.ds(3 * far, 3)], dst.at[0, 6:12, pl.ds(3 - far, 3)], to_far),
                send(phase, 2, src.at[6:12, pl.ds(3 * near_e, 3)], dst.at[0, 0:6, pl.ds(3 - near_e, 3)], to_e),
            ]
        return [send(phase, 3, src.at[0:6, 3:9], dst.at[1, 6:12], to_w)]

    def outward(phase, group, value, res, dst):
        res[group] = value
        if group == 0:
            sends = [
                send(phase, 0, res.at[0, 0:6, pl.ds(3 - far, 3)], dst.at[6:12, pl.ds(3 * far, 3)], to_w_from),
                send(phase, 1, res.at[0, 6:12, pl.ds(3 - far, 3)], dst.at[0:6, pl.ds(3 * far, 3)], to_from),
                send(phase, 2, res.at[0, 0:6, pl.ds(3 - near, 3)], dst.at[6:12, pl.ds(3 * near, 3)], to_w),
            ]
            dst[0:6, pl.ds(3 * near, 3)] = res[0, 6:12, pl.ds(3 - near, 3)]
        else:
            sends = [send(phase, 3, res.at[1, 6:12], dst.at[0:6, 3:9], to_e)]
            dst[6:12, 3:9] = value[0:6]
        return sends

    tok_sends = {group: inward(0, group, tokens, win_tok) for group in ORDER}
    go_sends = {group: inward(1, group, grad_out, win_go) for group in ORDER}

    low = lax.broadcasted_iota(jnp.int32, (WIN, PAIR), 1) < HALF
    gain1 = gain1_ref[...].astype(F32).reshape(1, D)
    gain2 = gain2_ref[...].astype(F32).reshape(1, D)

    def both(pair):
        zero = jnp.zeros_like(pair)
        return jnp.concatenate([jnp.where(low, pair, zero), jnp.where(low, zero, pair)], 0)

    def to_windows(rows, grid):
        wide = rows.astype(F32)
        columns = []
        for tile in range(TILES):
            grid[tile] = wide[:, tile * PAIR : tile * PAIR + PAIR]
            columns.append(
                jnp.concatenate([grid[tile, pl.ds(level, POS, stride=LEV), :] for level in LEVEL_ORDER], 0)
            )
        return jnp.concatenate(columns, 1)

    def from_windows(value, grid):
        columns = []
        for tile in range(TILES):
            for place, level in enumerate(LEVEL_ORDER):
                part = value[place * POS : place * POS + POS, tile * PAIR : tile * PAIR + PAIR]
                grid[tile, pl.ds(level, POS, stride=LEV), :] = part
            columns.append(grid[tile].astype(BF16))
        return jnp.concatenate(columns, 1).reshape(LON, LAT, LEV, D)

    spans = [slice(window * WIN, window * WIN + WIN) for window in range(2)]
    lanes = [slice(pair * PAIR, pair * PAIR + PAIR) for pair in range(4)]
    k_lanes = [slice(D + pair * PAIR, D + pair * PAIR + PAIR) for pair in range(4)]
    v_lanes = [slice(2 * D + pair * PAIR, 2 * D + pair * PAIR + PAIR) for pair in range(4)]
    head_rows = [slice(head * HALF, head * HALF + HALF) for head in range(8)]
    result_sends = []

    def forward(group):
        own_tok[group].wait()
        for copy in tok_sends[group]:
            copy.wait_recv()
        rows = to_windows(win_tok[group].reshape(ROWS, D), grid_tok)
        rows_in[group] = rows
        unit, scales[group] = norm_unit(rows)
        units[group] = unit
        normed = (unit * gain1).astype(BF16)
        if group == ORDER[0]:
            qkv_copy.wait()
        q = dot(normed, wqkv[:, 0:D]).astype(BF16)
        qkv[group, :, 0:D] = q * jnp.asarray(0.125, BF16)
        yield
        qkv[group, :, D : 2 * D] = dot(normed, wqkv[:, D : 2 * D]).astype(BF16)
        yield
        v = dot(normed, wqkv[:, 2 * D : 3 * D]).astype(BF16)
        qkv[group, :, 2 * D : 3 * D] = v
        for window in range(2):
            v_t[group, window] = v[spans[window]].T
        yield
        scores = {}
        for window in range(2):
            for pair in range(4):
                k_pair = qkv[group, spans[window], k_lanes[pair]]
                scores[window, pair] = dot_nt(both(k_pair), qkv[group, spans[window], lanes[pair]])
            yield
        weights = {}
        for window in range(2):
            for head in range(8):
                row = head % 2 * WIN
                score = scores[window, head // 2][row : row + WIN] + bias[group, window]
                expo = jnp.exp(score - jnp.max(score, 0, keepdims=True))
                prob = (expo * (1.0 / jnp.sum(expo, 0, keepdims=True))).astype(BF16)
                probs[group, window, head] = prob
                weights[window, head] = prob
                if head % 4 == 3:
                    yield
        for window in range(2):
            for head in range(8):
                mixed = dot(v_t[group, window, head_rows[head]], weights[window, head])
                turned[group, window, head_rows[head]] = mixed.astype(BF16)
            yield
        for window in range(2):
            att[group, spans[window]] = turned[group, window].T
        yield

    def tail(group):
        if group == ORDER[0]:
            for copy in tail_copies:
                copy.wait()
        mid = (rows_in[group] + dot(att[group], wproj[...])).astype(BF16)
        unit, inv_std = norm_unit(mid.astype(F32))
        normed = (unit * gain2).astype(BF16)
        yield
        own_go[group].wait()
        for copy in go_sends[group]:
            copy.wait_recv()
        grad_wide = to_windows(win_go[group].reshape(ROWS, D), grid_go)
        grad_rows = grad_wide.astype(BF16)
        yield
        for part in range(4):
            span = slice(part * 512, part * 512 + 512)
            grad_hidden = dot_nt(grad_rows, wdown[span, :])
            x = dot(normed, wup[:, span])
            c = math.sqrt(2.0 / math.pi)
            square = x * x
            cdf = 0.5 + 0.5 * jnp.tanh(x * (c + (c * 0.044715) * square))
            active = x * cdf
            act[group, :, span] = active.astype(BF16)
            slope = cdf * (1.0 + (x - active) * (2.0 * c + (6.0 * c * 0.044715) * square))
            gpre[group, :, span] = (slope * grad_hidden).astype(BF16)
            yield
        value = from_windows(mid.astype(F32) + dot(act[group], wdown[...]), grid_out)
        result_sends.extend(outward(2, group, value, out_res, out_ref))
        yield
        grad_normed = dot_nt(gpre[group], wup[...])
        grad_mid = (grad_wide + norm_grad(grad_normed, unit, inv_std, gain2)).astype(BF16)
        gmid[group] = grad_mid
        yield
        att[group] = dot_nt(grad_mid, wproj[...]).astype(BF16)
        yield

    def backward(group):
        for window in range(2):
            k_t[group, window] = qkv[group, spans[window], D : 2 * D].T
        yield
        grad_probs = {}
        for window in range(2):
            for pair in range(4):
                v_pair = qkv[group, spans[window], v_lanes[pair]]
                grad_probs[window, pair] = dot_nt(both(v_pair), att[group, spans[window], lanes[pair]])
            yield
        for window in range(2):
            for pair in range(4):
                prob = probs[group, window, 2 * pair : 2 * pair + 2].reshape(2 * WIN, WIN)
                grad_v = dot(prob, att[group, spans[window], lanes[pair]])
                gqkv[group, spans[window], v_lanes[pair]] = jnp.where(low, grad_v[:WIN], grad_v[WIN:]).astype(BF16)
            yield
        grad_scores = {}
        for window in range(2):
            for head in range(8):
                row = head % 2 * WIN
                wide = probs[group, window, head].astype(F32)
                grad_prob = grad_probs[window, head // 2][row : row + WIN]
                total = jnp.sum(grad_prob * wide, 0, keepdims=True)
                grad_scores[window, head] = (wide * (grad_prob - total)).astype(BF16)
                if head % 4 == 3:
                    yield
        for window in range(2):
            for head in range(8):
                grad_q = dot(k_t[group, window, head_rows[head]], grad_scores[window, head])
                turned[group, window, head_rows[head]] = (grad_q * 0.125).astype(BF16)
            yield
        for window in range(2):
            for pair in range(4):
                grad_score = jnp.concatenate([grad_scores[window, 2 * pair + h] for h in range(2)], 0)
                grad_k = dot(grad_score, qkv[group, spans[window], lanes[pair]])
                gqkv[group, spans[window], k_lanes[pair]] = jnp.where(low, grad_k[:WIN], grad_k[WIN:]).astype(BF16)
            yield
        for window in range(2):
            gqkv[group, spans[window], 0:D] = turned[group, window].T
        yield
        grad_normed = dot_nt(gqkv[group], wqkv[...])
        yield
        total = gmid[group].astype(F32) + norm_grad(grad_normed, units[group], scales[group], gain1)
        result = from_windows(total, grid_tgrad)
        result_sends.extend(outward(3, group, result, tgrad_res, tgrad_ref))
        yield

    def run(*works):
        turns = sorted(((step + 0.5) / count, n) for n, (_, count) in enumerate(works) for step in range(count))
        for _, n in turns:
            next(works[n][0], None)
        for work, _ in works:
            for _ in work:
                pass

    one, two = ORDER
    for group in ORDER:
        run((forward(group), 12))
        run((tail(group), 10))
        run((backward(group), 14))
    for copy in tok_sends[0] + tok_sends[1] + go_sends[0] + go_sends[1]:
        copy.wait_send()
    for copy in result_sends:
        copy.wait()


def write_out(out_ref, tgrad_ref, out_h, tgrad_h, sem):
    copies = []
    for which, (src, dst) in enumerate(((out_ref, out_h), (tgrad_ref, tgrad_h))):
        for part in range(3):
            span = slice(4 * part, 4 * part + 4)
            copies.append(pltpu.make_async_copy(src.at[span], dst.at[span], sem.at[which, part]))
    for copy in copies:
        copy.start()
    for copy in copies:
        copy.wait()


def on_device(
    nlon,
    nlat,
    tokens,
    grad_out,
    norm1_gain,
    qkv_weight,
    proj_weight,
    norm2_gain,
    up_weight,
    down_weight,
):
    any_spec = pl.BlockSpec(memory_space=pl.ANY)
    vmem_spec = pl.BlockSpec(memory_space=pltpu.VMEM)
    shape = jax.ShapeDtypeStruct(tokens.shape, BF16)
    block = (2, LON, LAT, LEV, D)
    in_vmem = pltpu.VMEM(tokens.shape, BF16)
    results = pl.pallas_call(
        functools.partial(kernel, nlon, nlat),
        out_shape=(in_vmem, in_vmem),
        in_specs=[any_spec, any_spec, vmem_spec, any_spec, any_spec, vmem_spec, any_spec, any_spec],
        out_specs=(vmem_spec, vmem_spec),
        scratch_shapes=[
            pltpu.VMEM((D, 3 * D), BF16),
            pltpu.VMEM((D, D), BF16),
            pltpu.VMEM((D, FF), BF16),
            pltpu.VMEM((FF, D), BF16),
            pltpu.VMEM((2, 2, WIN, WIN), F32),
            pltpu.VMEM(block, BF16),
            pltpu.VMEM(block, BF16),
            pltpu.VMEM(block, BF16),
            pltpu.VMEM(block, BF16),
            pltpu.VMEM((2, ROWS, 3 * D), BF16),
            pltpu.VMEM((2, 2, D, WIN), BF16),
            pltpu.VMEM((2, 2, D, WIN), BF16),
            pltpu.VMEM((2, 2, D, WIN), BF16),
            pltpu.VMEM((2, 2, 8, WIN, WIN), BF16),
            pltpu.VMEM((2, ROWS, 3 * D), BF16),
            pltpu.VMEM((2, ROWS, D), BF16),
            pltpu.VMEM((2, ROWS, FF), BF16),
            pltpu.VMEM((2, ROWS, FF), BF16),
            pltpu.VMEM((2, ROWS, D), BF16),
            pltpu.VMEM((2, ROWS, D), F32),
            pltpu.VMEM((2, ROWS, D), F32),
            pltpu.VMEM((2, ROWS, 1), F32),
            pltpu.VMEM((TILES, ROWS, PAIR), F32),
            pltpu.VMEM((TILES, ROWS, PAIR), F32),
            pltpu.VMEM((TILES, ROWS, PAIR), F32),
            pltpu.VMEM((TILES, ROWS, PAIR), F32),
            pltpu.SemaphoreType.DMA((4,)),
            pltpu.SemaphoreType.DMA((4,)),
            pltpu.SemaphoreType.DMA((4, 4)),
            pltpu.SemaphoreType.DMA((4, 4)),
        ],
        compiler_params=pltpu.CompilerParams(
            collective_id=0, has_side_effects=True, vmem_limit_bytes=56 * 1024 * 1024
        ),
        cost_estimate=pl.CostEstimate(
            flops=8_000_000_000, bytes_accessed=9_000_000, transcendentals=2_000_000
        ),
    )(
        tokens,
        grad_out,
        norm1_gain,
        qkv_weight,
        proj_weight,
        norm2_gain,
        up_weight,
        down_weight,
    )
    return pl.pallas_call(
        write_out,
        out_shape=(shape, shape),
        in_specs=[vmem_spec, vmem_spec],
        out_specs=(any_spec, any_spec),
        scratch_shapes=[pltpu.SemaphoreType.DMA((2, 3))],
        compiler_params=pltpu.CompilerParams(vmem_limit_bytes=8 * 1024 * 1024),
    )(*results)


def solution(mesh):
    grid = P("lon", "lat", None, None)
    return jax.shard_map(
        functools.partial(on_device, mesh.shape["lon"], mesh.shape["lat"]),
        mesh=mesh,
        in_specs=(grid, grid) + (P(),) * 6,
        out_specs=(grid, grid),
        check_vma=False,
    )
```

```python
import functools
import math

import jax
import jax.numpy as jnp
from jax import lax
from jax.experimental import pallas as pl
from jax.experimental.pallas import tpu as pltpu
from jax.sharding import PartitionSpec as P

MESH = pl.DeviceIdType.MESH
F32 = jnp.float32
BF16 = jnp.bfloat16
EPS = 1e-05
LON, LAT, LEV, D = 12, 6, 4, 512
POS = LON * LAT
ROWS = POS * LEV
WIN = ROWS // 2
FF = 2048
LEVEL_ORDER = (1, 2, 3, 0)
PAIR = 128
TILES = D // PAIR
ORDER = (1, 0)
HALF = 64


def dot(a, b):
    return jnp.dot(a, b, preferred_element_type=F32)


def dot_nt(a, b):
    return lax.dot_general(a, b, (((1,), (1,)), ((), ())), preferred_element_type=F32)


def norm_unit(x):
    centre = x - jnp.mean(x, -1, keepdims=True)
    inv_std = lax.rsqrt(jnp.mean(centre * centre, -1, keepdims=True) + EPS)
    return centre * inv_std, inv_std


def norm_grad(upstream, unit, inv_std, gain):
    scaled = upstream * gain
    return inv_std * (
        scaled
        - jnp.mean(scaled, -1, keepdims=True)
        - unit * jnp.mean(scaled * unit, -1, keepdims=True)
    )


def kernel(
    nlon,
    nlat,
    tokens,
    grad_out,
    gain1_ref,
    wqkv_h,
    wproj_h,
    gain2_ref,
    wup_h,
    wdown_h,
    out_ref,
    tgrad_ref,
    wqkv,
    wproj,
    wup,
    wdown,
    bias,
    win_tok,
    win_go,
    out_res,
    tgrad_res,
    qkv,
    k_t,
    v_t,
    turned,
    probs,
    gqkv,
    att,
    act,
    gpre,
    gmid,
    rows_in,
    units,
    scales,
    grid_tok,
    grid_go,
    grid_out,
    grid_tgrad,
    wsem,
    lsem,
    ssem,
    rsem,
):
    lon = lax.axis_index("lon")
    lat = lax.axis_index("lat")
    east, west = lax.rem(lon + 1, nlon), lax.rem(lon + nlon - 1, nlon)
    north, south = lax.rem(lat + 1, nlat), lax.rem(lat + nlat - 1, nlat)

    def column(index):
        odd = lax.rem(index, 2)
        near, far = 3 * odd, 3 - 3 * odd
        return near, far, odd * south + (1 - odd) * north

    near, far, far_to = column(lon)
    near_e, far_e, far_to_e = column(east)
    far_from = north + south - far_to
    to_e, to_w = (east, lat), (west, lat)
    to_far, to_from = (lon, far_to), (lon, far_from)
    to_e_far, to_w_from = (east, far_to_e), (west, far_from)

    barrier = pltpu.get_barrier_semaphore()
    for device in (to_e, to_w, to_far, to_from, to_e_far, to_w_from):
        pl.semaphore_signal(barrier, inc=1, device_id=device, device_id_type=MESH)

    def load(src, dst, sem):
        copy = pltpu.make_async_copy(src, dst, sem)
        copy.start()
        return copy

    def load_own(group, src, dst, sem):
        if group == 0:
            return load(src.at[0:6, pl.ds(3 * near, 3)], dst.at[0, 6:12, pl.ds(3 - near, 3)], sem)
        return load(src.at[6:12, 3:9], dst.at[1, 0:6], sem)

    own_tok = {group: load_own(group, tokens, win_tok, lsem.at[group]) for group in ORDER}
    qkv_copy = load(wqkv_h, wqkv, wsem.at[0])
    own_go = {group: load_own(group, grad_out, win_go, lsem.at[2 + group]) for group in ORDER}
    tail_copies = [
        load(wproj_h, wproj, wsem.at[1]),
        load(wup_h, wup, wsem.at[2]),
        load(wdown_h, wdown, wsem.at[3]),
    ]

    odd = lax.rem(lon, 2)
    edge = (lat == odd * (nlat - 1)).astype(jnp.int32)
    row = lax.broadcasted_iota(jnp.int32, (WIN, WIN), 0)
    col = lax.broadcasted_iota(jnp.int32, (WIN, WIN), 1)
    levels = ((row >= POS) != (col >= POS)).astype(jnp.int32)
    half_r = (lax.rem(row, LAT) >= LAT // 2).astype(jnp.int32)
    half_c = (lax.rem(col, LAT) >= LAT // 2).astype(jnp.int32)
    across = (half_r != half_c).astype(jnp.int32) * edge
    blocked = ((across, levels + across), (jnp.zeros_like(levels), levels))
    for group in range(2):
        for window in range(2):
            bias[group, window] = jnp.where(blocked[group][window] > 0, -1e30, 0.0)

    pl.semaphore_wait(barrier, 6)

    def send(phase, slot, src, dst, device):
        copy = pltpu.make_async_remote_copy(
            src_ref=src,
            dst_ref=dst,
            send_sem=ssem.at[phase, slot],
            recv_sem=rsem.at[phase, slot],
            device_id=device,
            device_id_type=MESH,
        )
        copy.start()
        return copy

    def inward(phase, group, src, dst):
        if group == 0:
            return [
                send(phase, 0, src.at[6:12, pl.ds(3 * far_e, 3)], dst.at[0, 0:6, pl.ds(3 - far_e, 3)], to_e_far),
                send(phase, 1, src.at[0:6, pl.ds(3 * far, 3)], dst.at[0, 6:12, pl.ds(3 - far, 3)], to_far),
                send(phase, 2, src.at[6:12, pl.ds(3 * near_e, 3)], dst.at[0, 0:6, pl.ds(3 - near_e, 3)], to_e),
            ]
        return [send(phase, 3, src.at[0:6, 3:9], dst.at[1, 6:12], to_w)]

    def outward(phase, group, value, res, dst):
        res[group] = value
        if group == 0:
            sends = [
                send(phase, 0, res.at[0, 0:6, pl.ds(3 - far, 3)], dst.at[6:12, pl.ds(3 * far, 3)], to_w_from),
                send(phase, 1, res.at[0, 6:12, pl.ds(3 - far, 3)], dst.at[0:6, pl.ds(3 * far, 3)], to_from),
                send(phase, 2, res.at[0, 0:6, pl.ds(3 - near, 3)], dst.at[6:12, pl.ds(3 * near, 3)], to_w),
            ]
            dst[0:6, pl.ds(3 * near, 3)] = res[0, 6:12, pl.ds(3 - near, 3)]
        else:
            sends = [send(phase, 3, res.at[1, 6:12], dst.at[0:6, 3:9], to_e)]
            dst[6:12, 3:9] = value[0:6]
        return sends

    tok_sends = {group: inward(0, group, tokens, win_tok) for group in ORDER}
    go_sends = {group: inward(1, group, grad_out, win_go) for group in ORDER}

    low = lax.broadcasted_iota(jnp.int32, (WIN, PAIR), 1) < HALF
    gain1 = gain1_ref[...].astype(F32).reshape(1, D)
    gain2 = gain2_ref[...].astype(F32).reshape(1, D)

    def both(pair):
        zero = jnp.zeros_like(pair)
        return jnp.concatenate([jnp.where(low, pair, zero), jnp.where(low, zero, pair)], 0)

    def to_windows(rows, grid):
        wide = rows.astype(F32)
        columns = []
        for tile in range(TILES):
            grid[tile] = wide[:, tile * PAIR : tile * PAIR + PAIR]
            columns.append(
                jnp.concatenate([grid[tile, pl.ds(level, POS, stride=LEV), :] for level in LEVEL_ORDER], 0)
            )
        return jnp.concatenate(columns, 1)

    def from_windows(value, grid):
        columns = []
        for tile in range(TILES):
            for place, level in enumerate(LEVEL_ORDER):
                part = value[place * POS : place * POS + POS, tile * PAIR : tile * PAIR + PAIR]
                grid[tile, pl.ds(level, POS, stride=LEV), :] = part
            columns.append(grid[tile].astype(BF16))
        return jnp.concatenate(columns, 1).reshape(LON, LAT, LEV, D)

    spans = [slice(window * WIN, window * WIN + WIN) for window in range(2)]
    lanes = [slice(pair * PAIR, pair * PAIR + PAIR) for pair in range(4)]
    k_lanes = [slice(D + pair * PAIR, D + pair * PAIR + PAIR) for pair in range(4)]
    v_lanes = [slice(2 * D + pair * PAIR, 2 * D + pair * PAIR + PAIR) for pair in range(4)]
    head_rows = [slice(head * HALF, head * HALF + HALF) for head in range(8)]
    result_sends = []

    def forward(group):
        own_tok[group].wait()
        for copy in tok_sends[group]:
            copy.wait_recv()
        rows = to_windows(win_tok[group].reshape(ROWS, D), grid_tok)
        rows_in[group] = rows
        unit, scales[group] = norm_unit(rows)
        units[group] = unit
        normed = (unit * gain1).astype(BF16)
        if group == ORDER[0]:
            qkv_copy.wait()
        q = dot(normed, wqkv[:, 0:D]).astype(BF16)
        qkv[group, :, 0:D] = q * jnp.asarray(0.125, BF16)
        yield
        qkv[group, :, D : 2 * D] = dot(normed, wqkv[:, D : 2 * D]).astype(BF16)
        yield
        v = dot(normed, wqkv[:, 2 * D : 3 * D]).astype(BF16)
        qkv[group, :, 2 * D : 3 * D] = v
        for window in range(2):
            v_t[group, window] = v[spans[window]].T
        yield
        scores = {}
        for window in range(2):
            for pair in range(4):
                k_pair = qkv[group, spans[window], k_lanes[pair]]
                scores[window, pair] = dot_nt(both(k_pair), qkv[group, spans[window], lanes[pair]])
            yield
        weights = {}
        for window in range(2):
            for head in range(8):
                row = head % 2 * WIN
                score = scores[window, head // 2][row : row + WIN]
                if (group, window) != (1, 0):
                    score = score + bias[group, window]
                expo = jnp.exp(score - jnp.max(score, 0, keepdims=True))
                prob = (expo * (1.0 / jnp.sum(expo, 0, keepdims=True))).astype(BF16)
                probs[group, window, head] = prob
                weights[window, head] = prob
                if head % 4 == 3:
                    yield
        for window in range(2):
            for head in range(8):
                mixed = dot(v_t[group, window, head_rows[head]], weights[window, head])
                turned[group, window, head_rows[head]] = mixed.astype(BF16)
            yield
        for window in range(2):
            att[group, spans[window]] = turned[group, window].T
        yield

    def tail(group):
        if group == ORDER[0]:
            for copy in tail_copies:
                copy.wait()
        mid = (rows_in[group] + dot(att[group], wproj[...])).astype(BF16)
        unit, inv_std = norm_unit(mid.astype(F32))
        normed = (unit * gain2).astype(BF16)
        yield
        own_go[group].wait()
        for copy in go_sends[group]:
            copy.wait_recv()
        grad_wide = to_windows(win_go[group].reshape(ROWS, D), grid_go)
        grad_rows = grad_wide.astype(BF16)
        yield
        for part in range(4):
            span = slice(part * 512, part * 512 + 512)
            grad_hidden = dot_nt(grad_rows, wdown[span, :])
            x = dot(normed, wup[:, span])
            c = math.sqrt(2.0 / math.pi)
            square = x * x
            cdf = 0.5 + 0.5 * jnp.tanh(x * (c + (c * 0.044715) * square))
            active = x * cdf
            act[group, :, span] = active.astype(BF16)
            slope = cdf * (1.0 + (x - active) * (2.0 * c + (6.0 * c * 0.044715) * square))
            gpre[group, :, span] = (slope * grad_hidden).astype(BF16)
            yield
        value = from_windows(mid.astype(F32) + dot(act[group], wdown[...]), grid_out)
        result_sends.extend(outward(2, group, value, out_res, out_ref))
        yield
        grad_normed = dot_nt(gpre[group], wup[...])
        grad_mid = (grad_wide + norm_grad(grad_normed, unit, inv_std, gain2)).astype(BF16)
        gmid[group] = grad_mid
        yield
        att[group] = dot_nt(grad_mid, wproj[...]).astype(BF16)
        yield

    def backward(group):
        for window in range(2):
            k_t[group, window] = qkv[group, spans[window], D : 2 * D].T
        yield
        grad_probs = {}
        for window in range(2):
            for pair in range(4):
                v_pair = qkv[group, spans[window], v_lanes[pair]]
                grad_probs[window, pair] = dot_nt(both(v_pair), att[group, spans[window], lanes[pair]])
            yield
        for window in range(2):
            for pair in range(4):
                prob = probs[group, window, 2 * pair : 2 * pair + 2].reshape(2 * WIN, WIN)
                grad_v = dot(prob, att[group, spans[window], lanes[pair]])
                gqkv[group, spans[window], v_lanes[pair]] = jnp.where(low, grad_v[:WIN], grad_v[WIN:]).astype(BF16)
            yield
        grad_normed = dot_nt(gqkv[group, :, 2 * D : 3 * D], wqkv[:, 2 * D : 3 * D])
        yield
        grad_scores = {}
        for window in range(2):
            for head in range(8):
                row = head % 2 * WIN
                wide = probs[group, window, head].astype(F32)
                grad_prob = grad_probs[window, head // 2][row : row + WIN]
                total = jnp.sum(grad_prob * wide, 0, keepdims=True)
                grad_scores[window, head] = (wide * (grad_prob - total)).astype(BF16)
                if head % 4 == 3:
                    yield
        for window in range(2):
            for head in range(8):
                grad_q = dot(k_t[group, window, head_rows[head]], grad_scores[window, head])
                turned[group, window, head_rows[head]] = (grad_q * 0.125).astype(BF16)
            yield
        for window in range(2):
            for pair in range(4):
                grad_score = jnp.concatenate([grad_scores[window, 2 * pair + h] for h in range(2)], 0)
                grad_k = dot(grad_score, qkv[group, spans[window], lanes[pair]])
                gqkv[group, spans[window], k_lanes[pair]] = jnp.where(low, grad_k[:WIN], grad_k[WIN:]).astype(BF16)
            yield
        for window in range(2):
            gqkv[group, spans[window], 0:D] = turned[group, window].T
        yield
        grad_normed = grad_normed + dot_nt(gqkv[group, :, 0 : 2 * D], wqkv[:, 0 : 2 * D])
        yield
        total = gmid[group].astype(F32) + norm_grad(grad_normed, units[group], scales[group], gain1)
        result = from_windows(total, grid_tgrad)
        result_sends.extend(outward(3, group, result, tgrad_res, tgrad_ref))
        yield

    def run(*works):
        turns = sorted(((step + 0.5) / count, n) for n, (_, count) in enumerate(works) for step in range(count))
        for _, n in turns:
            next(works[n][0], None)
        for work, _ in works:
            for _ in work:
                pass

    one, two = ORDER
    for group in ORDER:
        run((forward(group), 12))
        run((tail(group), 10))
        run((backward(group), 14))
    for copy in tok_sends[0] + tok_sends[1] + go_sends[0] + go_sends[1]:
        copy.wait_send()
    for copy in result_sends:
        copy.wait()


def write_out(out_ref, tgrad_ref, out_h, tgrad_h, sem):
    copies = []
    for which, (src, dst) in enumerate(((out_ref, out_h), (tgrad_ref, tgrad_h))):
        for part in range(3):
            span = slice(4 * part, 4 * part + 4)
            copies.append(pltpu.make_async_copy(src.at[span], dst.at[span], sem.at[which, part]))
    for copy in copies:
        copy.start()
    for copy in copies:
        copy.wait()


def on_device(
    nlon,
    nlat,
    tokens,
    grad_out,
    norm1_gain,
    qkv_weight,
    proj_weight,
    norm2_gain,
    up_weight,
    down_weight,
):
    any_spec = pl.BlockSpec(memory_space=pl.ANY)
    vmem_spec = pl.BlockSpec(memory_space=pltpu.VMEM)
    shape = jax.ShapeDtypeStruct(tokens.shape, BF16)
    block = (2, LON, LAT, LEV, D)
    in_vmem = pltpu.VMEM(tokens.shape, BF16)
    results = pl.pallas_call(
        functools.partial(kernel, nlon, nlat),
        out_shape=(in_vmem, in_vmem),
        in_specs=[any_spec, any_spec, vmem_spec, any_spec, any_spec, vmem_spec, any_spec, any_spec],
        out_specs=(vmem_spec, vmem_spec),
        scratch_shapes=[
            pltpu.VMEM((D, 3 * D), BF16),
            pltpu.VMEM((D, D), BF16),
            pltpu.VMEM((D, FF), BF16),
            pltpu.VMEM((FF, D), BF16),
            pltpu.VMEM((2, 2, WIN, WIN), F32),
            pltpu.VMEM(block, BF16),
            pltpu.VMEM(block, BF16),
            pltpu.VMEM(block, BF16),
            pltpu.VMEM(block, BF16),
            pltpu.VMEM((2, ROWS, 3 * D), BF16),
            pltpu.VMEM((2, 2, D, WIN), BF16),
            pltpu.VMEM((2, 2, D, WIN), BF16),
            pltpu.VMEM((2, 2, D, WIN), BF16),
            pltpu.VMEM((2, 2, 8, WIN, WIN), BF16),
            pltpu.VMEM((2, ROWS, 3 * D), BF16),
            pltpu.VMEM((2, ROWS, D), BF16),
            pltpu.VMEM((2, ROWS, FF), BF16),
            pltpu.VMEM((2, ROWS, FF), BF16),
            pltpu.VMEM((2, ROWS, D), BF16),
            pltpu.VMEM((2, ROWS, D), F32),
            pltpu.VMEM((2, ROWS, D), F32),
            pltpu.VMEM((2, ROWS, 1), F32),
            pltpu.VMEM((TILES, ROWS, PAIR), F32),
            pltpu.VMEM((TILES, ROWS, PAIR), F32),
            pltpu.VMEM((TILES, ROWS, PAIR), F32),
            pltpu.VMEM((TILES, ROWS, PAIR), F32),
            pltpu.SemaphoreType.DMA((4,)),
            pltpu.SemaphoreType.DMA((4,)),
            pltpu.SemaphoreType.DMA((4, 4)),
            pltpu.SemaphoreType.DMA((4, 4)),
        ],
        compiler_params=pltpu.CompilerParams(
            collective_id=0, has_side_effects=True, vmem_limit_bytes=56 * 1024 * 1024
        ),
        cost_estimate=pl.CostEstimate(
            flops=8_000_000_000, bytes_accessed=9_000_000, transcendentals=2_000_000
        ),
    )(
        tokens,
        grad_out,
        norm1_gain,
        qkv_weight,
        proj_weight,
        norm2_gain,
        up_weight,
        down_weight,
    )
    return pl.pallas_call(
        write_out,
        out_shape=(shape, shape),
        in_specs=[vmem_spec, vmem_spec],
        out_specs=(any_spec, any_spec),
        scratch_shapes=[pltpu.SemaphoreType.DMA((2, 3))],
        compiler_params=pltpu.CompilerParams(vmem_limit_bytes=8 * 1024 * 1024),
    )(*results)


def solution(mesh):
    grid = P("lon", "lat", None, None)
    return jax.shard_map(
        functools.partial(on_device, mesh.shape["lon"], mesh.shape["lat"]),
        mesh=mesh,
        in_specs=(grid, grid) + (P(),) * 6,
        out_specs=(grid, grid),
        check_vma=False,
    )
```
